512 devices in a mesh: gx: 8 (over y, z_hi), gy: 8 (over x, core), gz: 8 (over z_lo).
Axes of the slice: x: 4, y: 4, z: 16 (z_hi: 2, z_lo: 8; z = z_hi * 8 + z_lo), core: 2. Of those that a mesh axis runs over, the one named last changes fastest.
Arguments:
- pressure_new: float32 [64, 256, 1024], P('gx', 'gy', 'gz'), may hold values from -6 to 6
- pressure_old: float32 [64, 256, 1024], P('gx', 'gy', 'gz'), may hold values from -6 to 6
- codes: int32 [64, 256, 1024], P('gx', 'gy', 'gz'), may hold values from 0 to 15
- loss_table: float32 [16], replicated, may hold values from 0.01 to 0.4
- receivers: int32 [3, 128], replicated, may hold values from 0 to 1023, as said below
Outputs:
- final_new: float32 [64, 256, 1024], P('gx', 'gy', 'gz')
- final_old: float32 [64, 256, 1024], P('gx', 'gy', 'gz')
- traces: float32 [8, 128], replicated
The draws below stay inside these ranges and needn't reach their ends.
Inputs may be any that keep to these rules, and one draw needn't show every extreme that they name: receivers[0, r] is below 64, receivers[1, r] below 256, receivers[2, r] below 1024.
All inputs are finite; a program needn't handle non-finite values.
Results may differ from the reference program's by a relative error of at most 0.00015.
Values sent between devices are 32-bit elements; how exact they have to be, the bound alone decides.
A program may use at most 64 MiB of HBM per device.

```python
import math
import jax
import jax.numpy as jnp
from jax import lax

STEPS = 8
MATERIALS = 16
RECEIVERS = 128
NX = 64
NY = 256
NZ = 1024


def draw_pressure_new(key, part):
    key = jax.random.fold_in(key, 11)
    return jax.random.truncated_normal(key, -4.0, 4.0, (NX, NY, NZ), jnp.float32)


def draw_pressure_old(key, part):
    key = jax.random.fold_in(key, 17)
    return jax.random.truncated_normal(key, -4.0, 4.0, (NX, NY, NZ), jnp.float32)


def draw_receivers(key, part):
    key = jax.random.fold_in(key, 29)
    limits = jnp.array([NX, NY, NZ], dtype=jnp.int32)[:, None]
    positions = jax.random.randint(key, (3, RECEIVERS), 0, limits, dtype=jnp.int32)
    positions = positions.at[:, 0].set(limits[:, 0] - 1)
    positions = positions.at[:, 1].set(0)
    return positions


def place_ends(values, rng, low, high):
    extent = values.shape
    spot = [jax.random.randint(jax.random.fold_in(rng, axis), (), 0, extent[axis]) for axis in range(len(extent))]
    values = values.at[tuple(spot)].set(low)
    longest = extent.index(max(extent))
    spot[longest] = (spot[longest] + 1) % extent[longest]
    return values.at[tuple(spot)].set(high)


def setup_inputs(seed: int = 0) -> dict:
    key_list = jax.random.split(jax.random.key(seed), 6)
    return {
        "pressure_new": draw_pressure_new(jax.random.fold_in(key_list[5], 71), 0),
        "pressure_old": draw_pressure_old(jax.random.fold_in(key_list[5], 71), 0),
        "codes": place_ends(jax.random.randint(key_list[2], (NX, NY, NZ), 0, MATERIALS), jax.random.fold_in(key_list[2], 1), 0, MATERIALS - 1).astype(jnp.int32),
        "loss_table": jnp.clip(jnp.exp(jax.random.uniform(key_list[3], (MATERIALS,), jnp.float32, math.log(0.01), math.log(0.4))), 0.01, 0.4),
        "receivers": draw_receivers(jax.random.fold_in(key_list[5], 71), 0),
    }


EDGE_PARAM = 0.1292
CORNER_PARAM = 0.0036
COURANT_SQUARED = 0.64
FACE_WEIGHT = COURANT_SQUARED * (1.0 - 4.0 * EDGE_PARAM + 4.0 * CORNER_PARAM)
EDGE_WEIGHT = COURANT_SQUARED * (EDGE_PARAM - 2.0 * CORNER_PARAM)
CORNER_WEIGHT = COURANT_SQUARED * CORNER_PARAM
CENTRE_WEIGHT = 2.0 * (1.0 - 3.0 * COURANT_SQUARED + 6.0 * COURANT_SQUARED * EDGE_PARAM - 4.0 * COURANT_SQUARED * CORNER_PARAM)


def pair_sum(values, axis):
    widths = [(0, 0), (0, 0), (0, 0)]
    widths[axis] = (1, 1)
    padded = jnp.pad(values, widths)
    length = values.shape[axis]
    return lax.slice_in_dim(padded, 2, length + 2, axis=axis) + lax.slice_in_dim(padded, 0, length, axis=axis)


def reference(pressure_new, pressure_old, codes, loss_table, receivers):
    damping = jnp.take(loss_table, codes, axis=0)
    current = pressure_new
    previous = pressure_old
    samples = []
    for step_index in range(STEPS):
        along_x = pair_sum(current, 0)
        along_y = pair_sum(current, 1)
        along_z = pair_sum(current, 2)
        face_sum = along_x + along_y + along_z
        plane_xy = pair_sum(along_x, 1)
        edge_sum = plane_xy + pair_sum(along_x, 2) + pair_sum(along_y, 2)
        corner_sum = pair_sum(plane_xy, 2)
        total = FACE_WEIGHT * face_sum + EDGE_WEIGHT * edge_sum + CORNER_WEIGHT * corner_sum + CENTRE_WEIGHT * current
        advanced = (total + (damping - 1.0) * previous) / (1.0 + damping)
        previous = current
        current = advanced
        samples.append(current[receivers[0], receivers[1], receivers[2]])
    return current, previous, jnp.stack(samples)
```

```python
import jax
import jax.numpy as jnp
from jax import lax
from jax.experimental import pallas as pl
from jax.experimental.pallas import tpu as pltpu
from jax.sharding import PartitionSpec as P

STEPS = 8
EDGE_PARAM = 0.1292
CORNER_PARAM = 0.0036
COURANT_SQUARED = 0.64
FACE_WEIGHT = COURANT_SQUARED * (1.0 - 4.0 * EDGE_PARAM + 4.0 * CORNER_PARAM)
EDGE_WEIGHT = COURANT_SQUARED * (EDGE_PARAM - 2.0 * CORNER_PARAM)
CORNER_WEIGHT = COURANT_SQUARED * CORNER_PARAM
CENTRE_WEIGHT = 2.0 * (
    1.0
    - 3.0 * COURANT_SQUARED
    + 6.0 * COURANT_SQUARED * EDGE_PARAM
    - 4.0 * COURANT_SQUARED * CORNER_PARAM
)

MESH = pl.DeviceIdType.MESH
F32 = jnp.float32
ARRAYS = 3
MAIN = 128
STRIP = 16
LOW, HIGH = 8, 24
TOP, BOTTOM = 8, 40


def kernel(
    new_ref, old_ref, codes_ref, table_ref, rec_ref,
    fnew_ref, fold_ref, traces_ref,
    damp, snd, sndo, rcv, rcvo, reg, inv, dm, hist, onehot,
    outs, outr, part, ztr, ptr,
    s_in, r_in, s_out, r_out, s_halo, r_halo, s_back, r_back, s_tz, r_tz, s_tp, r_tp,
):
    gx, gy, k = (lax.axis_index(a) for a in ("gx", "gy", "gz"))
    y, h = lax.div(gx, 2), lax.rem(gx, 2)
    z = h * 8 + k

    def at_z(place):
        place = lax.rem(place, 16)
        return (2 * y + lax.div(place, 8), gy, lax.rem(place, 8))

    def at_plane(place):
        place = lax.rem(place, 32)
        return (2 * lax.div(place, 8) + h, lax.rem(place, 8), k)

    here = y * 8 + gy

    barrier = pltpu.get_barrier_semaphore()

    def greet_z(i, carry):
        pl.semaphore_signal(barrier, 1, device_id=at_z(z + i), device_id_type=MESH)
        return carry

    def greet_plane(i, carry):
        pl.semaphore_signal(
            barrier, 1, device_id=at_plane(here + i), device_id_type=MESH
        )
        return carry

    lax.fori_loop(1, 16, greet_z, 0)
    lax.fori_loop(1, 32, greet_plane, 0)

    role = jnp.where((z >= 4) & (z < 12), 0, 1)
    kk = jnp.where(role == 0, z - 4, lax.rem(z + 4, 16))
    has_outer = jnp.where(role == 0, kk > 0, kk < 7)
    inner_at = 64 - 8 * role
    outer_at = 120 * (1 - role)

    lane = lax.broadcasted_iota(jnp.int32, (32, 128), 1)
    low_lanes = lane < 64
    slot = lax.broadcasted_iota(jnp.int32, (STRIP, 128), 1) // 8

    def look_up(p, carry):
        codes = codes_ref[p]
        value = jnp.zeros((32, 128), F32)
        for material in range(16):
            value = jnp.where(codes == material, table_ref[material], value)
        damp[p] = value
        return carry

    lax.fori_loop(0, 8, look_up, 0)

    for a, ref in enumerate((damp, old_ref, new_ref)):

        def pack_main(p, carry, a=a, ref=ref):
            first, second = ref[p], pltpu.roll(ref[p + 4], 64, 1)
            rows = pl.ds(pl.multiple_of(p * 32, 32), 32)
            snd[a, 0, rows, :] = jnp.where(low_lanes, first, second)
            snd[a, 1, rows, :] = jnp.where(low_lanes, second, first)
            return carry

        lax.fori_loop(0, 4, pack_main, 0)

        def pack_strips(p, strips, a=a, ref=ref):
            value = ref[p]
            done = []
            for strip, begin in zip(strips, (64, 56, 120, 0)):
                upper = pltpu.roll(value[:16], lax.rem(8 * p + 128 - begin, 128), 1)
                lower = pltpu.roll(value[16:], lax.rem(8 * p + 192 - begin, 128), 1)
                strip = jnp.where(slot == p, upper, strip)
                done.append(jnp.where(slot == p + 8, lower, strip))
            return tuple(done)

        zero = jnp.zeros((STRIP, 128), F32)
        strips = lax.fori_loop(0, 8, pack_strips, (zero,) * 4)
        snd[a, 0, MAIN : MAIN + STRIP, :] = strips[0]
        snd[a, 1, MAIN : MAIN + STRIP, :] = strips[1]
        sndo[0, a * STRIP : (a + 1) * STRIP, :] = strips[2]
        sndo[1, a * STRIP : (a + 1) * STRIP, :] = strips[3]

    def clear(ref, planes, rows):
        count = planes.stop - planes.start
        height = rows.stop - rows.start
        zeros = jnp.zeros((height, 128), F32)

        def one(p, carry):
            ref[planes.start + p, rows, :] = zeros
            return carry

        lax.fori_loop(0, count, one, 0)

    def clear_outside(refs):
        for here_, planes, rows in (
            (y == 0, slice(0, 8), slice(0, 48)),
            (y == 3, slice(24, 32), slice(0, 48)),
            (gy == 0, slice(0, 32), slice(0, 8)),
            (gy == 7, slice(0, 32), slice(40, 48)),
        ):

            @pl.when(here_)
            def _(planes=planes, rows=rows):
                for ref in refs:
                    clear(ref, planes, rows)

    clear_outside((reg.at[1], reg.at[2]))

    z_at = rec_ref[2:3, :] - kk * 128
    sub = lax.broadcasted_iota(jnp.int32, (128, 128), 0)
    mine = (sub == z_at) & (sub // 64 == role)
    onehot[...] = jnp.where(mine, 1.0, 0.0)
    x_at = rec_ref[0:1, :] - y * 16
    y_at = rec_ref[1:2, :] - gy * 32
    inside = (x_at >= 0) & (x_at < 16) & (y_at >= 0) & (y_at < 32)
    row_at = jnp.where(inside, x_at * 32 + y_at, -1)

    pl.semaphore_wait(barrier, 46)

    targets = (at_z(k + 4), at_z(k + 12))

    def to_middle(a, half):
        return pltpu.make_async_remote_copy(
            src_ref=snd.at[a, half],
            dst_ref=rcv.at[a, h],
            send_sem=s_in.at[a, half],
            recv_sem=r_in.at[a, h],
            device_id=targets[half],
            device_id_type=MESH,
        )

    def in_middle(a, source):
        return pltpu.make_async_remote_copy(
            src_ref=snd.at[a, 0],
            dst_ref=rcv.at[a, source],
            send_sem=s_in.at[a, 0],
            recv_sem=r_in.at[a, source],
            device_id=targets[0],
            device_id_type=MESH,
        )

    def outer(way, source):
        return pltpu.make_async_remote_copy(
            src_ref=sndo.at[way],
            dst_ref=rcvo.at[source],
            send_sem=s_out.at[way],
            recv_sem=r_out.at[source],
            device_id=at_z(k + 5) if way == 0 else at_z(k + 11),
            device_id_type=MESH,
        )

    outer_ways = (k < 7, k > 0)
    for way in range(2):

        @pl.when(outer_ways[way])
        def _(way=way):
            outer(way, h).start()

    for a in range(ARRAYS):
        for half in range(2):
            to_middle(a, half).start()

    main_lanes = lane // 64 == role
    inner_lanes = (lane >= inner_at) & (lane < inner_at + 8)
    outer_lanes = (lane >= outer_at) & (
        lane < outer_at + jnp.where(has_outer, 8, 0)
    )
    some_lanes = main_lanes | inner_lanes | outer_lanes

    def unpack(a, source):
        inner_strip = rcv[a, source, MAIN : MAIN + STRIP, :]
        outer_strip = rcvo[source, a * STRIP : (a + 1) * STRIP, :]

        def spread(strip, p, begin):
            upper = pltpu.roll(strip, lax.rem(begin + 128 - 8 * p, 128), 1)
            lower = pltpu.roll(strip, lax.rem(begin + 192 - 8 * p, 128), 1)
            return jnp.concatenate([upper, lower], axis=0)

        def one(p, carry):
            packed = rcv[a, source, pl.ds(pl.multiple_of(p * 32, 32), 32), :]
            for q, main in ((p, packed), (p + 4, pltpu.roll(packed, 64, 1))):
                value = jnp.where(main_lanes, main, 0.0)
                value = jnp.where(inner_lanes, spread(inner_strip, q, inner_at), value)
                value = jnp.where(outer_lanes, spread(outer_strip, q, outer_at), value)
                reg[a, LOW + source * 8 + q, TOP:BOTTOM, :] = value
            return carry

        lax.fori_loop(0, 4, one, 0)

    ways = [(i, j) for i in (-1, 0, 1) for j in (-1, 0, 1) if (i, j) != (0, 0)]
    x_from = {-1: (8, 8), 0: (8, 16), 1: (16, 8)}
    x_to = {-1: (24, 8), 0: (8, 16), 1: (0, 8)}
    y_from = {-1: (8, 8), 0: (8, 32), 1: (32, 8)}
    y_to = {-1: (40, 8), 0: (8, 32), 1: (0, 8)}
    there_x = {-1: y > 0, 0: None, 1: y < 3}
    there_y = {-1: gy > 0, 0: None, 1: gy < 7}

    def exists(i, j):
        if there_x[i] is None:
            return there_y[j]
        if there_y[j] is None:
            return there_x[i]
        return there_x[i] & there_y[j]

    def halo(a, n):
        i, j = ways[n]
        (xf, xn), (yf, yn) = x_from[i], y_from[j]
        (xt, _), (yt, _) = x_to[i], y_to[j]
        return pltpu.make_async_remote_copy(
            src_ref=reg.at[a, pl.ds(xf, xn), pl.ds(yf, yn), :],
            dst_ref=reg.at[a, pl.ds(xt, xn), pl.ds(yt, yn), :],
            send_sem=s_halo.at[a, n],
            recv_sem=r_halo.at[a, n],
            device_id=(gx + 2 * i, gy + j, k),
            device_id_type=MESH,
        )

    def send_halos(a):
        for n, way in enumerate(ways):

            @pl.when(exists(*way))
            def _(n=n):
                halo(a, n).start()

    def left_halos(a):
        for n, way in enumerate(ways):

            @pl.when(exists(*way))
            def _(n=n):
                halo(a, n).wait_send()

    def wait_halos(a):
        for n, (i, j) in enumerate(ways):

            @pl.when(exists(-i, -j))
            def _(n=n):
                halo(a, n).wait_recv()

    def coefficients():
        lanes = jnp.concatenate([some_lanes, some_lanes[:16]], axis=0)

        def one(p, carry):
            d = reg[0, p]
            scale = jnp.where(lanes, 1.0 / (1.0 + d), 0.0)
            inv[p] = scale
            dm[p] = jnp.where(lanes, (d - 1.0) * scale, 0.0)
            return carry

        lax.fori_loop(0, 32, one, 0)
        clear_outside((inv, dm))

    for source in range(2):

        @pl.when(has_outer)
        def _(source=source):
            outer(0, source).wait_recv()

    for a in range(ARRAYS):
        for source in range(2):
            in_middle(a, source).wait_recv()
            unpack(a, source)
        send_halos(a)
        if a == 1:
            wait_halos(0)
            coefficients()
    wait_halos(1)
    wait_halos(2)
    left_halos(1)

    def spread_plane(v):
        side = pltpu.roll(v, 1, 1) + pltpu.roll(v, 127, 1)
        a = CENTRE_WEIGHT * v + FACE_WEIGHT * side
        b = FACE_WEIGHT * v + EDGE_WEIGHT * side
        c = EDGE_WEIGHT * v + CORNER_WEIGHT * side
        own = a + (pltpu.roll(b, 1, 0) + pltpu.roll(b, 47, 0))
        next_ = b + (pltpu.roll(c, 1, 0) + pltpu.roll(c, 47, 0))
        return own, next_

    for step in range(1, STEPS + 1):
        cur, prev = (2, 1) if step % 2 else (1, 2)

        def one(i, carry, cur=cur, prev=prev):
            total, before = carry
            own, next_ = spread_plane(reg[cur, i])
            p = i - 1
            reg[prev, p] = (total + next_) * inv[p] + dm[p] * reg[prev, p]
            return own + before, next_

        if step == 2:
            left_halos(2)
        _, first = spread_plane(reg[cur, step - 1])
        own, second = spread_plane(reg[cur, step])
        lax.fori_loop(step + 1, 33 - step, one, (own + first, second))

        def keep(p, carry, prev=prev, step=step):
            rows = pl.ds(pl.multiple_of(p * 32, 32), 32)
            hist[step - 1, rows, :] = reg[prev, LOW + p, TOP:BOTTOM, :]
            return carry

        lax.fori_loop(0, 16, keep, 0)

    def to_home(level, source):
        return pltpu.make_async_remote_copy(
            src_ref=outs.at[level, source],
            dst_ref=outr.at[level, role],
            send_sem=s_back.at[level, source],
            recv_sem=r_back.at[level, role],
            device_id=at_z(kk + 8 * source),
            device_id_type=MESH,
        )

    def at_home(level, half):
        return pltpu.make_async_remote_copy(
            src_ref=outs.at[level, 0],
            dst_ref=outr.at[level, half],
            send_sem=s_back.at[level, 0],
            recv_sem=r_back.at[level, half],
            device_id=at_z(kk),
            device_id_type=MESH,
        )

    for level in range(2):
        for source in range(2):

            def pack_back(p, carry, level=level, source=source):
                begin = source * 256
                here_ = hist[6 + level, pl.ds(pl.multiple_of(begin + p * 32, 32), 32), :]
                late = hist[
                    6 + level, pl.ds(pl.multiple_of(begin + 128 + p * 32, 32), 32), :
                ]
                outs[level, source, pl.ds(pl.multiple_of(p * 32, 32), 32), :] = (
                    jnp.where(main_lanes, here_, pltpu.roll(late, 64, 1))
                )
                return carry

            lax.fori_loop(0, 4, pack_back, 0)
            to_home(level, source).start()

    row = lax.broadcasted_iota(jnp.int32, (512, 128), 0)

    def sample(step, carry):
        picked = lax.dot_general(
            hist[step],
            onehot[...],
            (((1,), (0,)), ((), ())),
            precision=lax.Precision.HIGHEST,
            preferred_element_type=F32,
        )
        picked = jnp.where(row == row_at, picked, 0.0)
        part[pl.ds(step, 1), :] = jnp.sum(picked, axis=0, keepdims=True)
        return carry

    lax.fori_loop(0, STEPS, sample, 0)

    def in_plane(i):
        return pltpu.make_async_remote_copy(
            src_ref=part,
            dst_ref=ptr.at[i],
            send_sem=s_tp.at[i],
            recv_sem=r_tp.at[i],
            device_id=at_plane(here + i),
            device_id_type=MESH,
        )

    def in_ring(i):
        return pltpu.make_async_remote_copy(
            src_ref=ztr.at[0],
            dst_ref=ztr.at[i],
            send_sem=s_tz.at[i],
            recv_sem=r_tz.at[i],
            device_id=at_z(z + i),
            device_id_type=MESH,
        )

    def start_all(make, count):
        def one(i, carry):
            make(i).start()
            return carry

        lax.fori_loop(1, count, one, 0)

    def sum_all(make, count, own, slots):
        def one(i, total):
            make(i).wait_recv()
            return total + slots[i]

        return lax.fori_loop(1, count, one, own)

    start_all(in_plane, 32)
    ztr[0] = sum_all(in_plane, 32, part[...], ptr)
    start_all(in_ring, 16)

    for level, ref in ((0, fold_ref), (1, fnew_ref)):
        for half in range(2):
            at_home(level, half).wait_recv()

        def unpack_home(p, carry, level=level, ref=ref):
            rows = pl.ds(pl.multiple_of(p * 32, 32), 32)
            left, right = outr[level, 0, rows, :], outr[level, 1, rows, :]
            ref[p] = jnp.where(low_lanes, left, right)
            ref[p + 4] = pltpu.roll(jnp.where(low_lanes, right, left), 64, 1)
            return carry

        lax.fori_loop(0, 4, unpack_home, 0)

    traces_ref[...] = sum_all(in_ring, 16, ztr[0], ztr)

    for a in range(ARRAYS):
        for half in range(2):
            to_middle(a, half).wait_send()
    for way in range(2):

        @pl.when(outer_ways[way])
        def _(way=way):
            outer(way, h).wait_send()

    left_halos(0)

    for level in range(2):
        for source in range(2):
            to_home(level, source).wait_send()

    def left_plane(i, carry):
        in_plane(i).wait_send()
        return carry

    def left_ring(i, carry):
        in_ring(i).wait_send()
        return carry

    lax.fori_loop(1, 32, left_plane, 0)
    lax.fori_loop(1, 16, left_ring, 0)


def on_device(pressure_new, pressure_old, codes, loss_table, receivers):
    vmem = pl.BlockSpec(memory_space=pltpu.VMEM)
    smem = pl.BlockSpec(memory_space=pltpu.SMEM)
    block = jax.ShapeDtypeStruct((8, 32, 128), F32)
    dma = pltpu.SemaphoreType.DMA
    return pl.pallas_call(
        kernel,
        out_shape=(block, block, jax.ShapeDtypeStruct((STEPS, 128), F32)),
        in_specs=[vmem, vmem, vmem, smem, vmem],
        out_specs=(vmem, vmem, vmem),
        scratch_shapes=[
            pltpu.VMEM((8, 32, 128), F32),
            pltpu.VMEM((ARRAYS, 2, MAIN + STRIP, 128), F32),
            pltpu.VMEM((2, ARRAYS * STRIP, 128), F32),
            pltpu.VMEM((ARRAYS, 2, MAIN + STRIP, 128), F32),
            pltpu.VMEM((2, ARRAYS * STRIP, 128), F32),
            pltpu.VMEM((ARRAYS, 32, 48, 128), F32),
            pltpu.VMEM((32, 48, 128), F32),
            pltpu.VMEM((32, 48, 128), F32),
            pltpu.VMEM((STEPS, 512, 128), F32),
            pltpu.VMEM((128, 128), F32),
            pltpu.VMEM((2, 2, MAIN, 128), F32),
            pltpu.VMEM((2, 2, MAIN, 128), F32),
            pltpu.VMEM((STEPS, 128), F32),
            pltpu.VMEM((16, STEPS, 128), F32),
            pltpu.VMEM((32, STEPS, 128), F32),
            dma((ARRAYS, 2)), dma((ARRAYS, 2)),
            dma((2,)), dma((2,)),
            dma((ARRAYS, 8)), dma((ARRAYS, 8)),
            dma((2, 2)), dma((2, 2)),
            dma((16,)), dma((16,)),
            dma((32,)), dma((32,)),
        ],
        compiler_params=pltpu.CompilerParams(
            collective_id=0, has_side_effects=True, vmem_limit_bytes=32 << 20
        ),
        name="fdtd",
    )(pressure_new, pressure_old, codes, loss_table, receivers)


def solution(mesh):
    in_specs = (P("gx", "gy", "gz"), P("gx", "gy", "gz"), P("gx", "gy", "gz"), P(), P())
    out_specs = (P("gx", "gy", "gz"), P("gx", "gy", "gz"), P())
    return jax.shard_map(
        on_device, mesh=mesh, in_specs=in_specs, out_specs=out_specs, check_vma=False
    )
```

```python
import jax
import jax.numpy as jnp
from jax import lax
from jax.experimental import pallas as pl
from jax.experimental.pallas import tpu as pltpu
from jax.sharding import PartitionSpec as P

STEPS = 8
EDGE_PARAM = 0.1292
CORNER_PARAM = 0.0036
COURANT_SQUARED = 0.64
FACE_WEIGHT = COURANT_SQUARED * (1.0 - 4.0 * EDGE_PARAM + 4.0 * CORNER_PARAM)
EDGE_WEIGHT = COURANT_SQUARED * (EDGE_PARAM - 2.0 * CORNER_PARAM)
CORNER_WEIGHT = COURANT_SQUARED * CORNER_PARAM
CENTRE_WEIGHT = 2.0 * (
    1.0
    - 3.0 * COURANT_SQUARED
    + 6.0 * COURANT_SQUARED * EDGE_PARAM
    - 4.0 * COURANT_SQUARED * CORNER_PARAM
)

CENTRE_SCALED = CENTRE_WEIGHT / EDGE_WEIGHT
FACE_SCALED = FACE_WEIGHT / EDGE_WEIGHT
CORNER_SCALED = CORNER_WEIGHT / EDGE_WEIGHT

MESH = pl.DeviceIdType.MESH
F32 = jnp.float32
UNROLL = 16
ARRAYS = 3
MAIN = 128
STRIP = 16
LOW, HIGH = 8, 24
TOP, BOTTOM = 8, 40


def kernel(
    new_hbm, old_hbm, codes_hbm, table_hbm, rec_hbm,
    fnew_ref, fold_ref, traces_ref,
    new_ref, old_ref, codes_ref, table_ref, rec_ref, places, turns,
    damp, snd, sndo, rcv, rcvo, reg_d, reg_old, reg_new, inv, dm, hist,
    outs, outr, part, ztr, ptr,
    s_load, s_in, r_in, s_out, r_out, s_halo, r_halo, s_back, r_back, s_tz, r_tz, s_tp, r_tp,
):
    gx, gy, k = (lax.axis_index(a) for a in ("gx", "gy", "gz"))
    y, h = lax.div(gx, 2), lax.rem(gx, 2)
    z = h * 8 + k

    def at_z(place):
        place = lax.rem(place, 16)
        return (2 * y + lax.div(place, 8), gy, lax.rem(place, 8))

    def at_plane(place):
        place = lax.rem(place, 32)
        return (2 * lax.div(place, 8) + h, lax.rem(place, 8), k)

    here = y * 8 + gy
    regs = (reg_d, reg_old, reg_new)

    loads = [
        pltpu.make_async_copy(source, target, s_load.at[n])
        for n, (source, target) in enumerate(
            (
                (codes_hbm, codes_ref),
                (table_hbm, table_ref),
                (old_hbm, old_ref),
                (new_hbm, new_ref),
                (rec_hbm, rec_ref),
            )
        )
    ]
    for load in loads:
        load.start()

    barrier = pltpu.get_barrier_semaphore()
    for i in (4, 12, 5, 11, 3, 13, 2, 14):
        pl.semaphore_signal(barrier, 1, device_id=at_z(z + i), device_id_type=MESH)

    def greet_plane(i, carry):
        pl.semaphore_signal(
            barrier, 1, device_id=at_plane(here + i), device_id_type=MESH
        )
        return carry

    lax.fori_loop(1, 32, greet_plane, 0)

    role = jnp.where((z >= 4) & (z < 12), 0, 1)
    kk = jnp.where(role == 0, z - 4, lax.rem(z + 4, 16))
    has_outer = jnp.where(role == 0, kk > 0, kk < 7)
    inner_at = 64 - 8 * role
    outer_at = 120 * (1 - role)

    lane = lax.broadcasted_iota(jnp.int32, (32, 128), 1)
    low_lanes = lane < 64
    slot = lax.broadcasted_iota(jnp.int32, (STRIP, 128), 1) // 8

    def look_up(p, carry):
        codes = codes_ref[p]
        value = jnp.zeros((32, 128), F32)
        for material in range(16):
            value = jnp.where(codes == material, table_ref[material], value)
        damp[p] = value
        return carry

    loads[0].wait()
    loads[1].wait()
    lax.fori_loop(0, 8, look_up, 0)

    def pack(a, ref):
        def pack_main(p, carry):
            first, second = ref[p], pltpu.roll(ref[p + 4], 64, 1)
            rows = pl.ds(pl.multiple_of(p * 32, 32), 32)
            snd[a, 0, rows, :] = jnp.where(low_lanes, first, second)
            snd[a, 1, rows, :] = jnp.where(low_lanes, second, first)
            return carry

        lax.fori_loop(0, 4, pack_main, 0)
        strips = [jnp.zeros((STRIP, 128), F32)] * 4
        for p in range(8):
            value = ref[p]
            for n, begin in enumerate((64, 56, 120, 0)):
                upper = pltpu.roll(value[:16], (8 * p + 128 - begin) % 128, 1)
                lower = pltpu.roll(value[16:], (8 * p + 192 - begin) % 128, 1)
                strips[n] = jnp.where(slot == p, upper, strips[n])
                strips[n] = jnp.where(slot == p + 8, lower, strips[n])
        snd[a, 0, MAIN : MAIN + STRIP, :] = strips[0]
        snd[a, 1, MAIN : MAIN + STRIP, :] = strips[1]
        sndo[a, 0] = strips[2]
        sndo[a, 1] = strips[3]

    targets = (at_z(k + 4), at_z(k + 12))

    def to_middle(a, half):
        return pltpu.make_async_remote_copy(
            src_ref=snd.at[a, half],
            dst_ref=rcv.at[a, h],
            send_sem=s_in.at[a, half],
            recv_sem=r_in.at[a, h],
            device_id=targets[half],
            device_id_type=MESH,
        )

    def in_middle(a, source):
        return pltpu.make_async_remote_copy(
            src_ref=snd.at[a, 0],
            dst_ref=rcv.at[a, source],
            send_sem=s_in.at[a, 0],
            recv_sem=r_in.at[a, source],
            device_id=targets[0],
            device_id_type=MESH,
        )

    def outer(a, way, source):
        return pltpu.make_async_remote_copy(
            src_ref=sndo.at[a, way],
            dst_ref=rcvo.at[a, source],
            send_sem=s_out.at[a, way],
            recv_sem=r_out.at[a, source],
            device_id=at_z(k + 5) if way == 0 else at_z(k + 11),
            device_id_type=MESH,
        )

    outer_ways = (k < 7, k > 0)
    for a, ref in enumerate((damp, old_ref, new_ref)):
        if a:
            loads[a + 1].wait()
        pack(a, ref)
        if a == 0:
            pl.semaphore_wait(barrier, 39)
        for way in range(2):

            @pl.when(outer_ways[way])
            def _(a=a, way=way):
                outer(a, way, h).start()

        for half in range(2):
            to_middle(a, half).start()

    def clear(ref, planes, rows):
        count = planes.stop - planes.start
        height = rows.stop - rows.start
        zeros = jnp.zeros((height, 128), F32)

        def one(p, carry):
            ref[planes.start + p, rows, :] = zeros
            return carry

        lax.fori_loop(0, count, one, 0)

    def clear_outside(refs):
        for here_, planes, rows in (
            (y == 0, slice(0, 8), slice(0, 48)),
            (y == 3, slice(24, 32), slice(0, 48)),
            (gy == 0, slice(0, 32), slice(0, 8)),
            (gy == 7, slice(0, 32), slice(40, 48)),
        ):

            @pl.when(here_)
            def _(planes=planes, rows=rows):
                for ref in refs:
                    clear(ref, planes, rows)

    clear_outside((reg_old, reg_new))

    loads[4].wait()

    def locate(r, carry):
        x_at = rec_ref[0, r] - y * 16
        y_at = rec_ref[1, r] - gy * 32
        z_at = rec_ref[2, r] - kk * 128
        inside = (x_at >= 0) & (x_at < 16) & (y_at >= 0) & (y_at < 32)
        inside &= (z_at >= role * 64) & (z_at < role * 64 + 64)
        places[r] = jnp.where(inside, x_at * 32 + y_at, 0)
        turns[r] = jnp.where(inside, lax.rem(r - z_at + 128, 128), -1)
        return carry

    lax.fori_loop(0, 128, locate, 0)

    main_lanes = lane // 64 == role
    inner_lanes = (lane >= inner_at) & (lane < inner_at + 8)
    outer_lanes = (lane >= outer_at) & (
        lane < outer_at + jnp.where(has_outer, 8, 0)
    )
    some_lanes = main_lanes | inner_lanes | outer_lanes

    def unpack(a, source):
        inner_strip = rcv[a, source, MAIN : MAIN + STRIP, :]
        outer_strip = rcvo[a, source]

        def spread(strip, p, begin):
            upper = pltpu.roll(strip, lax.rem(begin + 128 - 8 * p, 128), 1)
            lower = pltpu.roll(strip, lax.rem(begin + 192 - 8 * p, 128), 1)
            return jnp.concatenate([upper, lower], axis=0)

        def one(p, carry):
            packed = rcv[a, source, pl.ds(pl.multiple_of(p * 32, 32), 32), :]
            for q, main in ((p, packed), (p + 4, pltpu.roll(packed, 64, 1))):
                value = jnp.where(main_lanes, main, 0.0)
                value = jnp.where(inner_lanes, spread(inner_strip, q, inner_at), value)
                value = jnp.where(outer_lanes, spread(outer_strip, q, outer_at), value)
                regs[a][LOW + source * 8 + q, TOP:BOTTOM, :] = value
            return carry

        lax.fori_loop(0, 4, one, 0)

    ways = [(i, j) for i in (-1, 0, 1) for j in (-1, 0, 1) if (i, j) != (0, 0)]
    x_from = {-1: (8, 8), 0: (8, 16), 1: (16, 8)}
    x_to = {-1: (24, 8), 0: (8, 16), 1: (0, 8)}
    y_from = {-1: (8, 8), 0: (8, 32), 1: (32, 8)}
    y_to = {-1: (40, 8), 0: (8, 32), 1: (0, 8)}
    there_x = {-1: y > 0, 0: None, 1: y < 3}
    there_y = {-1: gy > 0, 0: None, 1: gy < 7}

    def exists(i, j):
        if there_x[i] is None:
            return there_y[j]
        if there_y[j] is None:
            return there_x[i]
        return there_x[i] & there_y[j]

    def halo(a, n):
        i, j = ways[n]
        (xf, xn), (yf, yn) = x_from[i], y_from[j]
        (xt, _), (yt, _) = x_to[i], y_to[j]
        return pltpu.make_async_remote_copy(
            src_ref=regs[a].at[pl.ds(xf, xn), pl.ds(yf, yn), :],
            dst_ref=regs[a].at[pl.ds(xt, xn), pl.ds(yt, yn), :],
            send_sem=s_halo.at[a, n],
            recv_sem=r_halo.at[a, n],
            device_id=(gx + 2 * i, gy + j, k),
            device_id_type=MESH,
        )

    def send_halos(a):
        for n, way in enumerate(ways):

            @pl.when(exists(*way))
            def _(n=n):
                halo(a, n).start()

    def left_halos(a):
        for n, way in enumerate(ways):

            @pl.when(exists(*way))
            def _(n=n):
                halo(a, n).wait_send()

    def wait_halos(a):
        for n, (i, j) in enumerate(ways):

            @pl.when(exists(-i, -j))
            def _(n=n):
                halo(a, n).wait_recv()

    def coefficients():
        lanes = jnp.concatenate([some_lanes, some_lanes[:16]], axis=0)

        def one(p, carry):
            d = reg_d[p]
            scale = jnp.where(lanes, 1.0 / (1.0 + d), 0.0)
            inv[p] = EDGE_WEIGHT * scale
            dm[p] = jnp.where(lanes, (d - 1.0) * scale, 0.0)
            return carry

        lax.fori_loop(0, 32, one, 0)
        clear_outside((inv, dm))

    for a in range(ARRAYS):
        for source in range(2):

            @pl.when(has_outer)
            def _(a=a, source=source):
                outer(a, 0, source).wait_recv()

            in_middle(a, source).wait_recv()
            unpack(a, source)
        send_halos(a)
        if a == 1:
            wait_halos(0)
            coefficients()
    wait_halos(1)
    wait_halos(2)
    left_halos(1)

    def to_home(level, source):
        return pltpu.make_async_remote_copy(
            src_ref=outs.at[level, source],
            dst_ref=outr.at[level, role],
            send_sem=s_back.at[level, source],
            recv_sem=r_back.at[level, role],
            device_id=at_z(kk + 8 * source),
            device_id_type=MESH,
        )

    def at_home(level, half):
        return pltpu.make_async_remote_copy(
            src_ref=outs.at[level, 0],
            dst_ref=outr.at[level, half],
            send_sem=s_back.at[level, 0],
            recv_sem=r_back.at[level, half],
            device_id=at_z(kk),
            device_id_type=MESH,
        )

    def send_back(level, field):
        for source in range(2):

            def pack_back(p, carry, source=source):
                first = field[LOW + source * 8 + p, TOP:BOTTOM, :]
                second = field[LOW + source * 8 + 4 + p, TOP:BOTTOM, :]
                outs[level, source, pl.ds(pl.multiple_of(p * 32, 32), 32), :] = (
                    jnp.where(main_lanes, first, pltpu.roll(second, 64, 1))
                )
                return carry

            lax.fori_loop(0, 4, pack_back, 0)
            to_home(level, source).start()

    def spread_plane(v):
        side = pltpu.roll(v, 1, 1) + pltpu.roll(v, 127, 1)
        return (
            CENTRE_SCALED * v + FACE_SCALED * side,
            FACE_SCALED * v + side,
            v + CORNER_SCALED * side,
        )

    for step in range(1, STEPS + 1):
        cur, prev = (reg_new, reg_old) if step % 2 else (reg_old, reg_new)

        def one(p, carry, cur=cur, prev=prev):
            total, rows, b, c = carry
            a_next, b_next, c_next = spread_plane(cur[p + 1])
            rows = rows + c_next
            total = total + b_next + (pltpu.roll(rows, 1, 0) + pltpu.roll(rows, 47, 0))
            prev[p] = total * inv[p] + dm[p] * prev[p]
            return a_next + b, b_next + c, b_next, c_next

        def several(n, carry, one=one, step=step):
            for u in range(UNROLL):
                carry = one(step + n * UNROLL + u, carry)
            return carry

        if step == 2:
            left_halos(2)
        _, b, c = spread_plane(cur[step - 1])
        a_next, b_next, c_next = spread_plane(cur[step])
        carry = (a_next + b, b_next + c, b_next, c_next)
        loops, rest = divmod(32 - 2 * step, UNROLL)
        carry = lax.fori_loop(0, loops, several, carry)
        for p in range(32 - step - rest, 32 - step):
            carry = one(p, carry)

        if step >= STEPS - 1:
            send_back(step - STEPS + 1, prev)

        def keep(p, carry, prev=prev, step=step):
            rows = pl.ds(p * 256 + step - 1, 32, stride=8)
            hist.reshape(512 * STEPS, 128)[rows, :] = prev[LOW + p, TOP:BOTTOM, :]
            return carry

        lax.fori_loop(0, 16, keep, 0)

    lanes8 = lax.broadcasted_iota(jnp.int32, (STEPS, 128), 1)

    def sample(n, picked):
        for u in range(8):
            r = n * 8 + u
            turn = turns[r]
            rows = pltpu.roll(hist[places[r]], jnp.maximum(turn, 0), 1)
            picked = jnp.where(lanes8 == jnp.where(turn >= 0, r, -1), rows, picked)
        return picked

    part[...] = lax.fori_loop(0, 16, sample, jnp.zeros((STEPS, 128), F32))

    def in_plane(i):
        return pltpu.make_async_remote_copy(
            src_ref=part,
            dst_ref=ptr.at[i],
            send_sem=s_tp.at[i],
            recv_sem=r_tp.at[i],
            device_id=at_plane(here + i),
            device_id_type=MESH,
        )

    def in_ring(i):
        return pltpu.make_async_remote_copy(
            src_ref=ztr.at[0],
            dst_ref=ztr.at[i],
            send_sem=s_tz.at[i],
            recv_sem=r_tz.at[i],
            device_id=at_z(z + i),
            device_id_type=MESH,
        )

    def start_all(make, count):
        def one(i, carry):
            make(i).start()
            return carry

        lax.fori_loop(1, count, one, 0)

    def sum_all(make, count, own, slots):
        def one(i, total):
            make(i).wait_recv()
            return total + slots[i]

        return lax.fori_loop(1, count, one, own)

    start_all(in_plane, 32)
    ztr[0] = sum_all(in_plane, 32, part[...], ptr)
    start_all(in_ring, 16)

    for level, ref in ((0, fold_ref), (1, fnew_ref)):
        for half in range(2):
            at_home(level, half).wait_recv()

        def unpack_home(p, carry, level=level, ref=ref):
            rows = pl.ds(pl.multiple_of(p * 32, 32), 32)
            left, right = outr[level, 0, rows, :], outr[level, 1, rows, :]
            ref[p] = jnp.where(low_lanes, left, right)
            ref[p + 4] = pltpu.roll(jnp.where(low_lanes, right, left), 64, 1)
            return carry

        lax.fori_loop(0, 4, unpack_home, 0)

    traces_ref[...] = sum_all(in_ring, 16, ztr[0], ztr)

    for a in range(ARRAYS):
        for half in range(2):
            to_middle(a, half).wait_send()
        for way in range(2):

            @pl.when(outer_ways[way])
            def _(a=a, way=way):
                outer(a, way, h).wait_send()

    left_halos(0)

    for level in range(2):
        for source in range(2):
            to_home(level, source).wait_send()

    def left_plane(i, carry):
        in_plane(i).wait_send()
        return carry

    def left_ring(i, carry):
        in_ring(i).wait_send()
        return carry

    lax.fori_loop(1, 32, left_plane, 0)
    lax.fori_loop(1, 16, left_ring, 0)


def on_device(pressure_new, pressure_old, codes, loss_table, receivers):
    vmem = pl.BlockSpec(memory_space=pltpu.VMEM)
    anywhere = pl.BlockSpec(memory_space=pl.ANY)
    block = jax.ShapeDtypeStruct((8, 32, 128), F32)
    dma = pltpu.SemaphoreType.DMA
    return pl.pallas_call(
        kernel,
        out_shape=(block, block, jax.ShapeDtypeStruct((STEPS, 128), F32)),
        in_specs=[anywhere] * 5,
        out_specs=(vmem, vmem, vmem),
        scratch_shapes=[
            pltpu.VMEM((8, 32, 128), F32),
            pltpu.VMEM((8, 32, 128), F32),
            pltpu.VMEM((8, 32, 128), jnp.int32),
            pltpu.SMEM((16,), F32),
            pltpu.SMEM((3, 128), jnp.int32),
            pltpu.SMEM((128,), jnp.int32),
            pltpu.SMEM((128,), jnp.int32),
            pltpu.VMEM((8, 32, 128), F32),
            pltpu.VMEM((ARRAYS, 2, MAIN + STRIP, 128), F32),
            pltpu.VMEM((ARRAYS, 2, STRIP, 128), F32),
            pltpu.VMEM((ARRAYS, 2, MAIN + STRIP, 128), F32),
            pltpu.VMEM((ARRAYS, 2, STRIP, 128), F32),
            pltpu.VMEM((32, 48, 128), F32),
            pltpu.VMEM((32, 48, 128), F32),
            pltpu.VMEM((32, 48, 128), F32),
            pltpu.VMEM((32, 48, 128), F32),
            pltpu.VMEM((32, 48, 128), F32),
            pltpu.VMEM((512, STEPS, 128), F32),
            pltpu.VMEM((2, 2, MAIN, 128), F32),
            pltpu.VMEM((2, 2, MAIN, 128), F32),
            pltpu.VMEM((STEPS, 128), F32),
            pltpu.VMEM((16, STEPS, 128), F32),
            pltpu.VMEM((32, STEPS, 128), F32),
            dma((5,)),
            dma((ARRAYS, 2)), dma((ARRAYS, 2)),
            dma((ARRAYS, 2)), dma((ARRAYS, 2)),
            dma((ARRAYS, 8)), dma((ARRAYS, 8)),
            dma((2, 2)), dma((2, 2)),
            dma((16,)), dma((16,)),
            dma((32,)), dma((32,)),
        ],
        compiler_params=pltpu.CompilerParams(
            collective_id=0, has_side_effects=True, vmem_limit_bytes=60 << 20
        ),
        name="fdtd",
    )(pressure_new, pressure_old, codes, loss_table, receivers)


def solution(mesh):
    in_specs = (P("gx", "gy", "gz"), P("gx", "gy", "gz"), P("gx", "gy", "gz"), P(), P())
    out_specs = (P("gx", "gy", "gz"), P("gx", "gy", "gz"), P())
    return jax.shard_map(
        on_device, mesh=mesh, in_specs=in_specs, out_specs=out_specs, check_vma=False
    )
```

```python
import jax
import jax.numpy as jnp
from jax import lax
from jax.experimental import pallas as pl
from jax.experimental.pallas import tpu as pltpu
from jax.sharding import PartitionSpec as P

STEPS = 8
EDGE_PARAM = 0.1292
CORNER_PARAM = 0.0036
COURANT_SQUARED = 0.64
FACE_WEIGHT = COURANT_SQUARED * (1.0 - 4.0 * EDGE_PARAM + 4.0 * CORNER_PARAM)
EDGE_WEIGHT = COURANT_SQUARED * (EDGE_PARAM - 2.0 * CORNER_PARAM)
CORNER_WEIGHT = COURANT_SQUARED * CORNER_PARAM
CENTRE_WEIGHT = 2.0 * (
    1.0
    - 3.0 * COURANT_SQUARED
    + 6.0 * COURANT_SQUARED * EDGE_PARAM
    - 4.0 * COURANT_SQUARED * CORNER_PARAM
)

CENTRE_SCALED = CENTRE_WEIGHT / EDGE_WEIGHT
FACE_SCALED = FACE_WEIGHT / EDGE_WEIGHT
CORNER_SCALED = CORNER_WEIGHT / EDGE_WEIGHT

MESH = pl.DeviceIdType.MESH
F32 = jnp.float32
UNROLL = 16
ARRAYS = 3
MAIN = 128
STRIP = 16
LOW, HIGH = 8, 24
TOP, BOTTOM = 8, 40


def add_up(terms):
    while len(terms) > 1:
        terms = [sum(terms[i : i + 2]) for i in range(0, len(terms), 2)]
    return terms[0]


def kernel(
    new_hbm, old_hbm, codes_hbm, table_hbm, rec_hbm,
    outr, ztr,
    new_ref, old_ref, codes_ref, table_ref, rec_ref, places, turns,
    damp, snd, sndo, rcv, rcvo, reg_d, reg_old, reg_new, inv, dm, hist,
    outs, part, zsum, ptr,
    s_load, s_in, r_in, s_out, r_out, s_halo, r_halo, s_back, r_back, s_tz, r_tz, s_tp, r_tp, s_own,
):
    gx, gy, k = (lax.axis_index(a) for a in ("gx", "gy", "gz"))
    y, h = lax.div(gx, 2), lax.rem(gx, 2)
    z = h * 8 + k

    def at_z(place):
        place = lax.rem(place, 16)
        return (2 * y + lax.div(place, 8), gy, lax.rem(place, 8))

    def turned(place, by, size):
        place = place + by
        return jnp.where(place >= size, place - size, place)

    y_of = [2 * turned(y, i, 4) + h for i in range(4)]
    gy_of = [turned(gy, i, 8) for i in range(8)]
    plane = [(y_of[i], gy_of[j], k) for i in range(4) for j in range(8)]
    ring = []
    for i in range(16):
        place = turned(z, i, 16)
        upper = place >= 8
        ring.append(
            (2 * y + jnp.where(upper, 1, 0), gy, jnp.where(upper, place - 8, place))
        )
    plane_order = [i * 8 + j for i in (2, 1, 3, 0) for j in (4, 3, 5, 2, 6, 1, 7, 0)][:-1]
    ring_order = [8, 7, 9, 6, 10, 5, 11, 4, 12, 3, 13, 2, 14, 1, 15]

    regs = (reg_d, reg_old, reg_new)

    loads = [
        pltpu.make_async_copy(source, target, s_load.at[n])
        for n, (source, target) in enumerate(
            (
                (codes_hbm, codes_ref),
                (table_hbm, table_ref),
                (old_hbm, old_ref),
                (new_hbm, new_ref),
                (rec_hbm, rec_ref),
            )
        )
    ]
    for load in loads:
        load.start()

    barrier = pltpu.get_barrier_semaphore()
    for i in (4, 12, 5, 11, 3, 13, 2, 14):
        pl.semaphore_signal(barrier, 1, device_id=at_z(z + i), device_id_type=MESH)

    for i in plane_order:
        pl.semaphore_signal(barrier, 1, device_id=plane[i], device_id_type=MESH)

    role = jnp.where((z >= 4) & (z < 12), 0, 1)
    kk = jnp.where(role == 0, z - 4, lax.rem(z + 4, 16))
    has_outer = jnp.where(role == 0, kk > 0, kk < 7)
    inner_at = 64 - 8 * role
    outer_at = 120 * (1 - role)

    lane = lax.broadcasted_iota(jnp.int32, (32, 128), 1)
    low_lanes = lane < 64
    slot = lax.broadcasted_iota(jnp.int32, (STRIP, 128), 1) // 8

    def look_up(p, carry):
        codes = codes_ref[p]
        value = jnp.zeros((32, 128), F32)
        for material in range(16):
            value = jnp.where(codes == material, table_ref[material], value)
        damp[p] = value
        return carry

    loads[0].wait()
    loads[1].wait()
    lax.fori_loop(0, 8, look_up, 0)

    def pack(a, ref):
        def pack_main(p, carry):
            first, second = ref[p], pltpu.roll(ref[p + 4], 64, 1)
            rows = pl.ds(pl.multiple_of(p * 32, 32), 32)
            snd[a, 0, rows, :] = jnp.where(low_lanes, first, second)
            snd[a, 1, rows, :] = jnp.where(low_lanes, second, first)
            return carry

        lax.fori_loop(0, 4, pack_main, 0)
        strips = [jnp.zeros((STRIP, 128), F32)] * 4
        for p in range(8):
            value = ref[p]
            for n, begin in enumerate((64, 56, 120, 0)):
                upper = pltpu.roll(value[:16], (8 * p + 128 - begin) % 128, 1)
                lower = pltpu.roll(value[16:], (8 * p + 192 - begin) % 128, 1)
                strips[n] = jnp.where(slot == p, upper, strips[n])
                strips[n] = jnp.where(slot == p + 8, lower, strips[n])
        snd[a, 0, MAIN : MAIN + STRIP, :] = strips[0]
        snd[a, 1, MAIN : MAIN + STRIP, :] = strips[1]
        sndo[a, 0] = strips[2]
        sndo[a, 1] = strips[3]

    targets = (at_z(k + 4), at_z(k + 12))

    def to_middle(a, half):
        return pltpu.make_async_remote_copy(
            src_ref=snd.at[a, half],
            dst_ref=rcv.at[a, h],
            send_sem=s_in.at[a, half],
            recv_sem=r_in.at[a, h],
            device_id=targets[half],
            device_id_type=MESH,
        )

    def in_middle(a, source):
        return pltpu.make_async_remote_copy(
            src_ref=snd.at[a, 0],
            dst_ref=rcv.at[a, source],
            send_sem=s_in.at[a, 0],
            recv_sem=r_in.at[a, source],
            device_id=targets[0],
            device_id_type=MESH,
        )

    def outer(a, way, source):
        return pltpu.make_async_remote_copy(
            src_ref=sndo.at[a, way],
            dst_ref=rcvo.at[a, source],
            send_sem=s_out.at[a, way],
            recv_sem=r_out.at[a, source],
            device_id=at_z(k + 5) if way == 0 else at_z(k + 11),
            device_id_type=MESH,
        )

    outer_ways = (k < 7, k > 0)
    for a, ref in enumerate((damp, old_ref, new_ref)):
        if a:
            loads[a + 1].wait()
        pack(a, ref)
        if a == 0:
            pl.semaphore_wait(barrier, 39)
        if a == 2:
            for half in range(2):
                to_middle(0, half).wait_send()
        for way in range(2):

            @pl.when(outer_ways[way])
            def _(a=a, way=way):
                outer(a, way, h).start()

        for half in range(2):
            to_middle(a, half).start()

    def clear(ref, planes, rows):
        count = planes.stop - planes.start
        height = rows.stop - rows.start
        zeros = jnp.zeros((height, 128), F32)

        def one(p, carry):
            ref[planes.start + p, rows, :] = zeros
            return carry

        lax.fori_loop(0, count, one, 0)

    def clear_outside(refs):
        for here_, planes, rows in (
            (y == 0, slice(0, 8), slice(0, 48)),
            (y == 3, slice(24, 32), slice(0, 48)),
            (gy == 0, slice(0, 32), slice(0, 8)),
            (gy == 7, slice(0, 32), slice(40, 48)),
        ):

            @pl.when(here_)
            def _(planes=planes, rows=rows):
                for ref in refs:
                    clear(ref, planes, rows)

    clear_outside((reg_old, reg_new))

    loads[4].wait()

    def locate(r, carry):
        x_at = rec_ref[0, r] - y * 16
        y_at = rec_ref[1, r] - gy * 32
        z_at = rec_ref[2, r] - kk * 128
        inside = (x_at >= 0) & (x_at < 16) & (y_at >= 0) & (y_at < 32)
        inside &= (z_at >= role * 64) & (z_at < role * 64 + 64)
        places[r] = jnp.where(inside, x_at * 32 + y_at, 0)
        turns[r] = jnp.where(inside, lax.rem(r - z_at + 128, 128), -1)
        return carry

    lax.fori_loop(0, 128, locate, 0)

    main_lanes = lane // 64 == role
    inner_lanes = (lane >= inner_at) & (lane < inner_at + 8)
    outer_lanes = (lane >= outer_at) & (
        lane < outer_at + jnp.where(has_outer, 8, 0)
    )
    some_lanes = main_lanes | inner_lanes | outer_lanes

    def unpack(a, source):
        inner_strip = rcv[a, source, MAIN : MAIN + STRIP, :]
        outer_strip = rcvo[a, source]

        def spread(strip, p, begin):
            upper = pltpu.roll(strip, lax.rem(begin + 128 - 8 * p, 128), 1)
            lower = pltpu.roll(strip, lax.rem(begin + 192 - 8 * p, 128), 1)
            return jnp.concatenate([upper, lower], axis=0)

        def one(p, carry):
            packed = rcv[a, source, pl.ds(pl.multiple_of(p * 32, 32), 32), :]
            for q, main in ((p, packed), (p + 4, pltpu.roll(packed, 64, 1))):
                value = jnp.where(main_lanes, main, 0.0)
                value = jnp.where(inner_lanes, spread(inner_strip, q, inner_at), value)
                value = jnp.where(outer_lanes, spread(outer_strip, q, outer_at), value)
                regs[a][LOW + source * 8 + q, TOP:BOTTOM, :] = value
            return carry

        lax.fori_loop(0, 4, one, 0)

    ways = [(-1, -1), (-1, 1), (1, -1), (1, 1), (-1, 0), (1, 0), (0, -1), (0, 1)]
    x_from = {-1: (8, 8), 0: (8, 16), 1: (16, 8)}
    x_to = {-1: (24, 8), 0: (8, 16), 1: (0, 8)}
    y_from = {-1: (8, 8), 0: (8, 32), 1: (32, 8)}
    y_to = {-1: (40, 8), 0: (8, 32), 1: (0, 8)}
    there_x = {-1: y > 0, 0: None, 1: y < 3}
    there_y = {-1: gy > 0, 0: None, 1: gy < 7}

    def exists(i, j):
        if there_x[i] is None:
            return there_y[j]
        if there_y[j] is None:
            return there_x[i]
        return there_x[i] & there_y[j]

    def halo(a, n):
        i, j = ways[n]
        (xf, xn), (yf, yn) = x_from[i], y_from[j]
        (xt, _), (yt, _) = x_to[i], y_to[j]
        return pltpu.make_async_remote_copy(
            src_ref=regs[a].at[pl.ds(xf, xn), pl.ds(yf, yn), :],
            dst_ref=regs[a].at[pl.ds(xt, xn), pl.ds(yt, yn), :],
            send_sem=s_halo.at[a, n],
            recv_sem=r_halo.at[a, n],
            device_id=(gx + 2 * i, gy + j, k),
            device_id_type=MESH,
        )

    def send_halos(a):
        for n, way in enumerate(ways):

            @pl.when(exists(*way))
            def _(n=n):
                halo(a, n).start()

    def left_halos(a):
        for n, way in enumerate(ways):

            @pl.when(exists(*way))
            def _(n=n):
                halo(a, n).wait_send()

    def wait_halos(a):
        for n, (i, j) in enumerate(ways):

            @pl.when(exists(-i, -j))
            def _(n=n):
                halo(a, n).wait_recv()

    def coefficients():
        lanes = jnp.concatenate([some_lanes, some_lanes[:16]], axis=0)

        def one(p, carry):
            d = reg_d[p]
            scale = jnp.where(lanes, 1.0 / (1.0 + d), 0.0)
            inv[p] = EDGE_WEIGHT * scale
            dm[p] = jnp.where(lanes, (d - 1.0) * scale, 0.0)
            return carry

        lax.fori_loop(0, 32, one, 0)
        clear_outside((inv, dm))

    for a in range(ARRAYS):
        for source in range(2):

            @pl.when(has_outer)
            def _(a=a, source=source):
                outer(a, 0, source).wait_recv()

            in_middle(a, source).wait_recv()
            unpack(a, source)
        send_halos(a)
        if a == 1:
            wait_halos(0)
            coefficients()
    wait_halos(1)
    wait_halos(2)
    left_halos(1)

    def to_home(level, source):
        return pltpu.make_async_remote_copy(
            src_ref=outs.at[level, source],
            dst_ref=outr.at[level, role],
            send_sem=s_back.at[level, source],
            recv_sem=r_back.at[level, role],
            device_id=at_z(kk + 8 * source),
            device_id_type=MESH,
        )

    def at_home(level, half):
        return pltpu.make_async_remote_copy(
            src_ref=outs.at[level, 0],
            dst_ref=outr.at[level, half],
            send_sem=s_back.at[level, 0],
            recv_sem=r_back.at[level, half],
            device_id=at_z(kk),
            device_id_type=MESH,
        )

    def send_back(level, field):
        for source in range(2):

            def pack_back(p, carry, source=source):
                first = field[LOW + source * 8 + p, TOP:BOTTOM, :]
                second = field[LOW + source * 8 + 4 + p, TOP:BOTTOM, :]
                outs[level, source, pl.ds(pl.multiple_of(p * 32, 32), 32), :] = (
                    jnp.where(main_lanes, first, pltpu.roll(second, 64, 1))
                )
                return carry

            lax.fori_loop(0, 4, pack_back, 0)
            to_home(level, source).start()

    def spread_plane(v):
        side = pltpu.roll(v, 1, 1) + pltpu.roll(v, 127, 1)
        return (
            CENTRE_SCALED * v + FACE_SCALED * side,
            FACE_SCALED * v + side,
            v + CORNER_SCALED * side,
        )

    for step in range(1, STEPS + 1):
        cur, prev = (reg_new, reg_old) if step % 2 else (reg_old, reg_new)

        def one(p, carry, cur=cur, prev=prev):
            total, rows, b, c = carry
            a_next, b_next, c_next = spread_plane(cur[p + 1])
            rows = rows + c_next
            total = total + b_next + (pltpu.roll(rows, 1, 0) + pltpu.roll(rows, 47, 0))
            prev[p] = total * inv[p] + dm[p] * prev[p]
            return a_next + b, b_next + c, b_next, c_next

        def several(n, carry, one=one, step=step):
            for u in range(UNROLL):
                carry = one(step + n * UNROLL + u, carry)
            return carry

        if step == 2:
            left_halos(2)
        _, b, c = spread_plane(cur[step - 1])
        a_next, b_next, c_next = spread_plane(cur[step])
        carry = (a_next + b, b_next + c, b_next, c_next)
        loops, rest = divmod(32 - 2 * step, UNROLL)
        carry = lax.fori_loop(0, loops, several, carry)
        for p in range(32 - step - rest, 32 - step):
            carry = one(p, carry)

        if step >= STEPS - 1:
            send_back(step - STEPS + 1, prev)

        def keep(p, carry, prev=prev, step=step):
            rows = pl.ds(p * 256 + step - 1, 32, stride=8)
            hist.reshape(512 * STEPS, 128)[rows, :] = prev[LOW + p, TOP:BOTTOM, :]
            return carry

        lax.fori_loop(0, 16, keep, 0)

    lanes8 = lax.broadcasted_iota(jnp.int32, (STEPS, 128), 1)

    def sample(n, picked):
        for u in range(8):
            r = n * 8 + u
            turn = turns[r]
            rows = pltpu.roll(hist[places[r]], jnp.maximum(turn, 0), 1)
            picked = jnp.where(lanes8 == jnp.where(turn >= 0, r, -1), rows, picked)
        return picked

    part[...] = lax.fori_loop(0, 16, sample, jnp.zeros((STEPS, 128), F32))

    def in_plane(i):
        return pltpu.make_async_remote_copy(
            src_ref=part,
            dst_ref=ptr.at[i],
            send_sem=s_tp,
            recv_sem=r_tp,
            device_id=plane[i],
            device_id_type=MESH,
        )

    def in_ring(i):
        return pltpu.make_async_remote_copy(
            src_ref=zsum,
            dst_ref=ztr.at[i],
            send_sem=s_tz,
            recv_sem=r_tz,
            device_id=ring[i],
            device_id_type=MESH,
        )

    def whole(slots, send_sem, recv_sem, target):
        others = slots.at[pl.ds(1, slots.shape[0] - 1)]
        return pltpu.make_async_remote_copy(
            src_ref=others,
            dst_ref=others,
            send_sem=send_sem,
            recv_sem=recv_sem,
            device_id=target,
            device_id_type=MESH,
        )

    all_plane = whole(ptr, s_tp, r_tp, plane[1])
    all_ring = whole(ztr, s_tz, r_tz, ring[1])
    for i in plane_order:
        in_plane(i).start()
    all_plane.wait_recv()
    zsum[...] = add_up([part[...]] + [ptr[i] for i in range(1, 32)])
    own = pltpu.make_async_copy(zsum, ztr.at[0], s_own)
    own.start()
    for i in ring_order:
        in_ring(i).start()

    for level in range(2):
        for half in range(2):
            at_home(level, half).wait_recv()
    all_ring.wait_recv()
    own.wait()

    for a in range(ARRAYS):
        for half in range(2):
            if a > 0:
                to_middle(a, half).wait_send()
        for way in range(2):

            @pl.when(outer_ways[way])
            def _(a=a, way=way):
                outer(a, way, h).wait_send()

    left_halos(0)

    for level in range(2):
        for source in range(2):
            to_home(level, source).wait_send()

    all_plane.wait_send()
    all_ring.wait_send()


def hand_over(packed, sums, new, old, traces):
    low_lanes = lax.broadcasted_iota(jnp.int32, (32, 128), 1) < 64
    for level, ref in ((0, old), (1, new)):
        for p in range(4):
            rows = slice(p * 32, (p + 1) * 32)
            left, right = packed[level, 0, rows, :], packed[level, 1, rows, :]
            ref[p] = jnp.where(low_lanes, left, right)
            ref[p + 4] = pltpu.roll(jnp.where(low_lanes, right, left), 64, 1)
    traces[...] = add_up([sums[i] for i in range(16)])


def on_device(pressure_new, pressure_old, codes, loss_table, receivers):
    vmem = pl.BlockSpec(memory_space=pltpu.VMEM)
    anywhere = pl.BlockSpec(memory_space=pl.ANY)
    block = jax.ShapeDtypeStruct((8, 32, 128), F32)
    dma = pltpu.SemaphoreType.DMA
    shapes = (block, block, jax.ShapeDtypeStruct((STEPS, 128), F32))
    results = pl.pallas_call(
        kernel,
        out_shape=(
            jax.ShapeDtypeStruct((2, 2, MAIN, 128), F32),
            jax.ShapeDtypeStruct((16, STEPS, 128), F32),
        ),
        in_specs=[anywhere] * 5,
        out_specs=(anywhere, anywhere),
        scratch_shapes=[
            pltpu.VMEM((8, 32, 128), F32),
            pltpu.VMEM((8, 32, 128), F32),
            pltpu.VMEM((8, 32, 128), jnp.int32),
            pltpu.SMEM((16,), F32),
            pltpu.SMEM((3, 128), jnp.int32),
            pltpu.SMEM((128,), jnp.int32),
            pltpu.SMEM((128,), jnp.int32),
            pltpu.VMEM((8, 32, 128), F32),
            pltpu.VMEM((ARRAYS, 2, MAIN + STRIP, 128), F32),
            pltpu.VMEM((ARRAYS, 2, STRIP, 128), F32),
            pltpu.VMEM((ARRAYS, 2, MAIN + STRIP, 128), F32),
            pltpu.VMEM((ARRAYS, 2, STRIP, 128), F32),
            pltpu.VMEM((32, 48, 128), F32),
            pltpu.VMEM((32, 48, 128), F32),
            pltpu.VMEM((32, 48, 128), F32),
            pltpu.VMEM((32, 48, 128), F32),
            pltpu.VMEM((32, 48, 128), F32),
            pltpu.VMEM((512, STEPS, 128), F32),
            pltpu.VMEM((2, 2, MAIN, 128), F32),
            pltpu.VMEM((STEPS, 128), F32),
            pltpu.VMEM((STEPS, 128), F32),
            pltpu.VMEM((32, STEPS, 128), F32),
            dma((5,)),
            dma((ARRAYS, 2)), dma((ARRAYS, 2)),
            dma((ARRAYS, 2)), dma((ARRAYS, 2)),
            dma((ARRAYS, 8)), dma((ARRAYS, 8)),
            dma((2, 2)), dma((2, 2)),
            dma, dma, dma, dma, dma,
        ],
        compiler_params=pltpu.CompilerParams(
            collective_id=0, has_side_effects=True, vmem_limit_bytes=60 << 20
        ),
        name="fdtd",
    )(pressure_new, pressure_old, codes, loss_table, receivers)
    return pl.pallas_call(
        hand_over,
        out_shape=shapes,
        in_specs=[vmem] * 2,
        out_specs=(vmem,) * 3,
        name="hand_over",
    )(*results)


def solution(mesh):
    in_specs = (P("gx", "gy", "gz"), P("gx", "gy", "gz"), P("gx", "gy", "gz"), P(), P())
    out_specs = (P("gx", "gy", "gz"), P("gx", "gy", "gz"), P())
    return jax.shard_map(
        on_device, mesh=mesh, in_specs=in_specs, out_specs=out_specs, check_vma=False
    )
```

```python
import jax
import jax.numpy as jnp
from jax import lax
from jax.experimental import pallas as pl
from jax.experimental.pallas import tpu as pltpu
from jax.sharding import PartitionSpec as P

STEPS = 8
EDGE_PARAM = 0.1292
CORNER_PARAM = 0.0036
COURANT_SQUARED = 0.64
FACE_WEIGHT = COURANT_SQUARED * (1.0 - 4.0 * EDGE_PARAM + 4.0 * CORNER_PARAM)
EDGE_WEIGHT = COURANT_SQUARED * (EDGE_PARAM - 2.0 * CORNER_PARAM)
CORNER_WEIGHT = COURANT_SQUARED * CORNER_PARAM
CENTRE_WEIGHT = 2.0 * (
    1.0
    - 3.0 * COURANT_SQUARED
    + 6.0 * COURANT_SQUARED * EDGE_PARAM
    - 4.0 * COURANT_SQUARED * CORNER_PARAM
)

CENTRE_SCALED = CENTRE_WEIGHT / EDGE_WEIGHT
FACE_SCALED = FACE_WEIGHT / EDGE_WEIGHT
CORNER_SCALED = CORNER_WEIGHT / EDGE_WEIGHT

MESH = pl.DeviceIdType.MESH
F32 = jnp.float32
UNROLL = 16
ARRAYS = 3
MAIN = 128
STRIP = 16
LOW, HIGH = 8, 24
TOP, BOTTOM = 8, 40


def add_up(terms):
    while len(terms) > 1:
        terms = [sum(terms[i : i + 2]) for i in range(0, len(terms), 2)]
    return terms[0]


def kernel(
    new_hbm, old_hbm, codes_hbm, table_hbm, rec_hbm,
    outr, ztr,
    new_ref, old_ref, codes_ref, table_ref, rec_ref, places, turns,
    damp, snd, sndo, rcv, rcvo, reg_d, reg_old, reg_new, inv, dm, hist,
    outs, part, zsum, ptr,
    s_load, s_in, r_in, s_out, r_out, s_halo, r_halo, s_back, r_back, s_tz, r_tz, s_tp, r_tp, s_own, s_pass, r_pass,
):
    gx, gy, k = (lax.axis_index(a) for a in ("gx", "gy", "gz"))
    y, h = lax.div(gx, 2), lax.rem(gx, 2)
    z = h * 8 + k

    def at_z(place):
        place = lax.rem(place, 16)
        return (2 * y + lax.div(place, 8), gy, lax.rem(place, 8))

    def turned(place, by, size):
        place = place + by
        return jnp.where(place >= size, place - size, place)

    y_of = [2 * turned(y, i, 4) + h for i in range(4)]
    gy_of = [turned(gy, i, 8) for i in range(8)]
    plane = [(y_of[i], gy_of[j], k) for i in range(4) for j in range(8)]
    ring = []
    for i in range(16):
        place = turned(z, i, 16)
        upper = place >= 8
        ring.append(
            (2 * y + jnp.where(upper, 1, 0), gy, jnp.where(upper, place - 8, place))
        )
    plane_order = [i * 8 + j for i in (2, 1, 3, 0) for j in (4, 3, 5, 2, 6, 1, 7, 0)][:-1]
    ring_order = [8, 7, 9, 6, 10, 5, 11, 4, 12, 3, 13, 2, 14, 1, 15]

    regs = (reg_d, reg_old, reg_new)

    loads = [
        pltpu.make_async_copy(source, target, s_load.at[n])
        for n, (source, target) in enumerate(
            (
                (codes_hbm, codes_ref),
                (table_hbm, table_ref),
                (old_hbm, old_ref),
                (new_hbm, new_ref),
                (rec_hbm, rec_ref),
            )
        )
    ]
    for load in loads:
        load.start()

    barrier = pltpu.get_barrier_semaphore()
    for i in (4, 12, 5, 11, 3, 13, 2, 14):
        pl.semaphore_signal(barrier, 1, device_id=at_z(z + i), device_id_type=MESH)

    for i in plane_order:
        pl.semaphore_signal(barrier, 1, device_id=plane[i], device_id_type=MESH)

    role = jnp.where((z >= 4) & (z < 12), 0, 1)
    kk = jnp.where(role == 0, z - 4, lax.rem(z + 4, 16))
    has_outer = jnp.where(role == 0, kk > 0, kk < 7)
    inner_at = 64 - 8 * role
    outer_at = 120 * (1 - role)

    lane = lax.broadcasted_iota(jnp.int32, (32, 128), 1)
    low_lanes = lane < 64
    slot = lax.broadcasted_iota(jnp.int32, (STRIP, 128), 1) // 8

    def look_up(p, carry):
        codes = codes_ref[p]
        value = jnp.zeros((32, 128), F32)
        for material in range(16):
            value = jnp.where(codes == material, table_ref[material], value)
        damp[p] = value
        return carry

    loads[0].wait()
    loads[1].wait()
    lax.fori_loop(0, 8, look_up, 0)

    def pack(a, ref):
        def pack_main(p, carry):
            first, second = ref[p], pltpu.roll(ref[p + 4], 64, 1)
            rows = pl.ds(pl.multiple_of(p * 32, 32), 32)
            snd[a, 0, rows, :] = jnp.where(low_lanes, first, second)
            snd[a, 1, rows, :] = jnp.where(low_lanes, second, first)
            return carry

        lax.fori_loop(0, 4, pack_main, 0)
        strips = [jnp.zeros((STRIP, 128), F32)] * 4
        for p in range(8):
            value = ref[p]
            for n, begin in enumerate((64, 56, 120, 0)):
                upper = pltpu.roll(value[:16], (8 * p + 128 - begin) % 128, 1)
                lower = pltpu.roll(value[16:], (8 * p + 192 - begin) % 128, 1)
                strips[n] = jnp.where(slot == p, upper, strips[n])
                strips[n] = jnp.where(slot == p + 8, lower, strips[n])
        snd[a, 0, MAIN : MAIN + STRIP, :] = strips[0]
        snd[a, 1, MAIN : MAIN + STRIP, :] = strips[1]
        sndo[a, 0] = strips[2]
        sndo[a, 1] = strips[3]

    targets = (at_z(k + 4), at_z(k + 12))

    def to_middle(a, half):
        return pltpu.make_async_remote_copy(
            src_ref=snd.at[a, half],
            dst_ref=rcv.at[a, h],
            send_sem=s_in.at[a, half],
            recv_sem=r_in.at[a, h],
            device_id=targets[half],
            device_id_type=MESH,
        )

    def in_middle(a, source):
        return pltpu.make_async_remote_copy(
            src_ref=snd.at[a, 0],
            dst_ref=rcv.at[a, source],
            send_sem=s_in.at[a, 0],
            recv_sem=r_in.at[a, source],
            device_id=targets[0],
            device_id_type=MESH,
        )

    def outer(a, way, source):
        return pltpu.make_async_remote_copy(
            src_ref=sndo.at[a, way],
            dst_ref=rcvo.at[a, source],
            send_sem=s_out.at[a, way],
            recv_sem=r_out.at[a, source],
            device_id=at_z(k + 5) if way == 0 else at_z(k + 11),
            device_id_type=MESH,
        )

    outer_ways = (k < 7, k > 0)
    for a, ref in enumerate((damp, old_ref, new_ref)):
        if a:
            loads[a + 1].wait()
        pack(a, ref)
        if a == 0:
            pl.semaphore_wait(barrier, 39)
        if a == 2:
            for half in range(2):
                to_middle(0, half).wait_send()
        for way in range(2):

            @pl.when(outer_ways[way])
            def _(a=a, way=way):
                outer(a, way, h).start()

        for half in range(2):
            to_middle(a, half).start()

    def clear(ref, planes, rows):
        count = planes.stop - planes.start
        height = rows.stop - rows.start
        zeros = jnp.zeros((height, 128), F32)

        def one(p, carry):
            ref[planes.start + p, rows, :] = zeros
            return carry

        lax.fori_loop(0, count, one, 0)

    def clear_outside(refs):
        for here_, planes, rows in (
            (y == 0, slice(0, 8), slice(0, 48)),
            (y == 3, slice(24, 32), slice(0, 48)),
            (gy == 0, slice(0, 32), slice(0, 8)),
            (gy == 7, slice(0, 32), slice(40, 48)),
        ):

            @pl.when(here_)
            def _(planes=planes, rows=rows):
                for ref in refs:
                    clear(ref, planes, rows)

    clear_outside((reg_old, reg_new))

    loads[4].wait()

    def locate(r, carry):
        x_at = rec_ref[0, r] - y * 16
        y_at = rec_ref[1, r] - gy * 32
        z_at = rec_ref[2, r] - kk * 128
        inside = (x_at >= 0) & (x_at < 16) & (y_at >= 0) & (y_at < 32)
        inside &= (z_at >= role * 64) & (z_at < role * 64 + 64)
        places[r] = jnp.where(inside, x_at * 32 + y_at, 0)
        turns[r] = jnp.where(inside, lax.rem(r - z_at + 128, 128), -1)
        return carry

    lax.fori_loop(0, 128, locate, 0)

    main_lanes = lane // 64 == role
    inner_lanes = (lane >= inner_at) & (lane < inner_at + 8)
    outer_lanes = (lane >= outer_at) & (
        lane < outer_at + jnp.where(has_outer, 8, 0)
    )
    some_lanes = main_lanes | inner_lanes | outer_lanes

    plane_of = (8, 16, 0, 24)

    def unpack(a, source):
        inner_strip = rcv[a, source, MAIN : MAIN + STRIP, :]
        outer_strip = rcvo[a, source]

        def spread(strip, p, begin):
            upper = pltpu.roll(strip, lax.rem(begin + 128 - 8 * p, 128), 1)
            lower = pltpu.roll(strip, lax.rem(begin + 192 - 8 * p, 128), 1)
            return jnp.concatenate([upper, lower], axis=0)

        def one(p, carry):
            packed = rcv[a, source, pl.ds(pl.multiple_of(p * 32, 32), 32), :]
            for q, main in ((p, packed), (p + 4, pltpu.roll(packed, 64, 1))):
                value = jnp.where(main_lanes, main, 0.0)
                value = jnp.where(inner_lanes, spread(inner_strip, q, inner_at), value)
                value = jnp.where(outer_lanes, spread(outer_strip, q, outer_at), value)
                regs[a][plane_of[source] + q, TOP:BOTTOM, :] = value
            return carry

        lax.fori_loop(0, 4, one, 0)

    ways = [(-1, -1), (-1, 1), (1, -1), (1, 1), (0, -1), (0, 1)]
    x_from = {-1: (8, 8), 0: (8, 16), 1: (16, 8)}
    x_to = {-1: (24, 8), 0: (8, 16), 1: (0, 8)}
    y_from = {-1: (8, 8), 0: (8, 32), 1: (32, 8)}
    y_to = {-1: (40, 8), 0: (8, 32), 1: (0, 8)}
    there_x = {-1: y > 0, 0: None, 1: y < 3}
    there_y = {-1: gy > 0, 0: None, 1: gy < 7}

    def exists(i, j):
        if there_x[i] is None:
            return there_y[j]
        if there_y[j] is None:
            return there_x[i]
        return there_x[i] & there_y[j]

    def halo(a, n):
        i, j = ways[n]
        (xf, xn), (yf, yn) = x_from[i], y_from[j]
        (xt, _), (yt, _) = x_to[i], y_to[j]
        return pltpu.make_async_remote_copy(
            src_ref=regs[a].at[pl.ds(xf, xn), pl.ds(yf, yn), :],
            dst_ref=regs[a].at[pl.ds(xt, xn), pl.ds(yt, yn), :],
            send_sem=s_halo.at[a, n],
            recv_sem=r_halo.at[a, n],
            device_id=(gx + 2 * i, gy + j, k),
            device_id_type=MESH,
        )

    def pass_on(a, source):
        i = 2 * source - 1
        copies = []
        for n, ref in enumerate((rcv, rcvo)):
            copies.append(
                pltpu.make_async_remote_copy(
                    src_ref=ref.at[a, source],
                    dst_ref=ref.at[a, 3 - source],
                    send_sem=s_pass.at[a, source, n],
                    recv_sem=r_pass.at[a, 3 - source - 2, n],
                    device_id=(gx + 2 * i, gy, k),
                    device_id_type=MESH,
                )
            )
        return copies

    def each_pass(a, source, there, act):
        block, strip = pass_on(a, source)

        @pl.when(there & has_outer)
        def _():
            act(strip)

        @pl.when(there)
        def _():
            act(block)

    def send_pass(a, source):
        each_pass(a, source, y < 3 if source else y > 0, lambda copy: copy.start())

    def left_pass(a, source):
        each_pass(a, source, y < 3 if source else y > 0, lambda copy: copy.wait_send())

    def wait_pass(a, source):
        there = y > 0 if source else y < 3
        each_pass(a, source, there, lambda copy: copy.wait_recv())

        @pl.when(there)
        def _():
            unpack(a, 3 - source)

    def send_halos(a):
        for n, way in enumerate(ways):

            @pl.when(exists(*way))
            def _(n=n):
                halo(a, n).start()

    def left_halos(a):
        for n, way in enumerate(ways):

            @pl.when(exists(*way))
            def _(n=n):
                halo(a, n).wait_send()

    def wait_halos(a):
        for n, (i, j) in enumerate(ways):

            @pl.when(exists(-i, -j))
            def _(n=n):
                halo(a, n).wait_recv()

    def take_halos(a):
        for source in range(2):
            wait_pass(a, source)
        wait_halos(a)

    def coefficients():
        lanes = jnp.concatenate([some_lanes, some_lanes[:16]], axis=0)

        def one(p, carry):
            d = reg_d[p]
            scale = jnp.where(lanes, 1.0 / (1.0 + d), 0.0)
            inv[p] = EDGE_WEIGHT * scale
            dm[p] = jnp.where(lanes, (d - 1.0) * scale, 0.0)
            return carry

        lax.fori_loop(0, 32, one, 0)
        clear_outside((inv, dm))

    for a in range(ARRAYS):
        for source in range(2):

            @pl.when(has_outer)
            def _(a=a, source=source):
                outer(a, 0, source).wait_recv()

            in_middle(a, source).wait_recv()
            send_pass(a, source)
        for source in range(2):
            unpack(a, source)
        send_halos(a)
        if a == 1:
            take_halos(0)
            coefficients()
    take_halos(1)
    take_halos(2)
    left_halos(1)

    def to_home(level, source):
        return pltpu.make_async_remote_copy(
            src_ref=outs.at[level, source],
            dst_ref=outr.at[level, role],
            send_sem=s_back.at[level, source],
            recv_sem=r_back.at[level, role],
            device_id=at_z(kk + 8 * source),
            device_id_type=MESH,
        )

    def at_home(level, half):
        return pltpu.make_async_remote_copy(
            src_ref=outs.at[level, 0],
            dst_ref=outr.at[level, half],
            send_sem=s_back.at[level, 0],
            recv_sem=r_back.at[level, half],
            device_id=at_z(kk),
            device_id_type=MESH,
        )

    def send_back(level, field):
        for source in range(2):

            def pack_back(p, carry, source=source):
                first = field[LOW + source * 8 + p, TOP:BOTTOM, :]
                second = field[LOW + source * 8 + 4 + p, TOP:BOTTOM, :]
                outs[level, source, pl.ds(pl.multiple_of(p * 32, 32), 32), :] = (
                    jnp.where(main_lanes, first, pltpu.roll(second, 64, 1))
                )
                return carry

            lax.fori_loop(0, 4, pack_back, 0)
            to_home(level, source).start()

    def spread_plane(v):
        side = pltpu.roll(v, 1, 1) + pltpu.roll(v, 127, 1)
        return (
            CENTRE_SCALED * v + FACE_SCALED * side,
            FACE_SCALED * v + side,
            v + CORNER_SCALED * side,
        )

    for step in range(1, STEPS + 1):
        cur, prev = (reg_new, reg_old) if step % 2 else (reg_old, reg_new)

        def one(p, carry, cur=cur, prev=prev):
            total, rows, b, c = carry
            a_next, b_next, c_next = spread_plane(cur[p + 1])
            rows = rows + c_next
            total = total + b_next + (pltpu.roll(rows, 1, 0) + pltpu.roll(rows, 47, 0))
            prev[p] = total * inv[p] + dm[p] * prev[p]
            return a_next + b, b_next + c, b_next, c_next

        def several(n, carry, one=one, step=step):
            for u in range(UNROLL):
                carry = one(step + n * UNROLL + u, carry)
            return carry

        if step == 2:
            left_halos(2)
        _, b, c = spread_plane(cur[step - 1])
        a_next, b_next, c_next = spread_plane(cur[step])
        carry = (a_next + b, b_next + c, b_next, c_next)
        loops, rest = divmod(32 - 2 * step, UNROLL)
        carry = lax.fori_loop(0, loops, several, carry)
        for p in range(32 - step - rest, 32 - step):
            carry = one(p, carry)

        if step >= STEPS - 1:
            send_back(step - STEPS + 1, prev)

        def keep(p, carry, prev=prev, step=step):
            rows = pl.ds(p * 256 + step - 1, 32, stride=8)
            hist.reshape(512 * STEPS, 128)[rows, :] = prev[LOW + p, TOP:BOTTOM, :]
            return carry

        lax.fori_loop(0, 16, keep, 0)

    lanes8 = lax.broadcasted_iota(jnp.int32, (STEPS, 128), 1)

    def sample(n, picked):
        for u in range(8):
            r = n * 8 + u
            turn = turns[r]
            rows = pltpu.roll(hist[places[r]], jnp.maximum(turn, 0), 1)
            picked = jnp.where(lanes8 == jnp.where(turn >= 0, r, -1), rows, picked)
        return picked

    part[...] = lax.fori_loop(0, 16, sample, jnp.zeros((STEPS, 128), F32))

    def in_plane(i):
        return pltpu.make_async_remote_copy(
            src_ref=part,
            dst_ref=ptr.at[i],
            send_sem=s_tp,
            recv_sem=r_tp,
            device_id=plane[i],
            device_id_type=MESH,
        )

    def in_ring(i):
        return pltpu.make_async_remote_copy(
            src_ref=zsum,
            dst_ref=ztr.at[i],
            send_sem=s_tz,
            recv_sem=r_tz,
            device_id=ring[i],
            device_id_type=MESH,
        )

    def whole(slots, send_sem, recv_sem, target):
        others = slots.at[pl.ds(1, slots.shape[0] - 1)]
        return pltpu.make_async_remote_copy(
            src_ref=others,
            dst_ref=others,
            send_sem=send_sem,
            recv_sem=recv_sem,
            device_id=target,
            device_id_type=MESH,
        )

    all_plane = whole(ptr, s_tp, r_tp, plane[1])
    all_ring = whole(ztr, s_tz, r_tz, ring[1])
    for i in plane_order:
        in_plane(i).start()
    all_plane.wait_recv()
    zsum[...] = add_up([part[...]] + [ptr[i] for i in range(1, 32)])
    own = pltpu.make_async_copy(zsum, ztr.at[0], s_own)
    own.start()
    for i in ring_order:
        in_ring(i).start()

    for level in range(2):
        for half in range(2):
            at_home(level, half).wait_recv()
    all_ring.wait_recv()
    own.wait()

    for a in range(ARRAYS):
        for half in range(2):
            if a > 0:
                to_middle(a, half).wait_send()
        for way in range(2):

            @pl.when(outer_ways[way])
            def _(a=a, way=way):
                outer(a, way, h).wait_send()

    left_halos(0)
    for a in range(ARRAYS):
        for source in range(2):
            left_pass(a, source)

    for level in range(2):
        for source in range(2):
            to_home(level, source).wait_send()

    all_plane.wait_send()
    all_ring.wait_send()


def hand_over(packed, sums, new, old, traces):
    low_lanes = lax.broadcasted_iota(jnp.int32, (32, 128), 1) < 64
    for level, ref in ((0, old), (1, new)):
        for p in range(4):
            rows = slice(p * 32, (p + 1) * 32)
            left, right = packed[level, 0, rows, :], packed[level, 1, rows, :]
            ref[p] = jnp.where(low_lanes, left, right)
            ref[p + 4] = pltpu.roll(jnp.where(low_lanes, right, left), 64, 1)
    traces[...] = add_up([sums[i] for i in range(16)])


def on_device(pressure_new, pressure_old, codes, loss_table, receivers):
    vmem = pl.BlockSpec(memory_space=pltpu.VMEM)
    anywhere = pl.BlockSpec(memory_space=pl.ANY)
    block = jax.ShapeDtypeStruct((8, 32, 128), F32)
    dma = pltpu.SemaphoreType.DMA
    shapes = (block, block, jax.ShapeDtypeStruct((STEPS, 128), F32))
    results = pl.pallas_call(
        kernel,
        out_shape=(
            jax.ShapeDtypeStruct((2, 2, MAIN, 128), F32),
            jax.ShapeDtypeStruct((16, STEPS, 128), F32),
        ),
        in_specs=[anywhere] * 5,
        out_specs=(anywhere, anywhere),
        scratch_shapes=[
            pltpu.VMEM((8, 32, 128), F32),
            pltpu.VMEM((8, 32, 128), F32),
            pltpu.VMEM((8, 32, 128), jnp.int32),
            pltpu.SMEM((16,), F32),
            pltpu.SMEM((3, 128), jnp.int32),
            pltpu.SMEM((128,), jnp.int32),
            pltpu.SMEM((128,), jnp.int32),
            pltpu.VMEM((8, 32, 128), F32),
            pltpu.VMEM((ARRAYS, 2, MAIN + STRIP, 128), F32),
            pltpu.VMEM((ARRAYS, 2, STRIP, 128), F32),
            pltpu.VMEM((ARRAYS, 4, MAIN + STRIP, 128), F32),
            pltpu.VMEM((ARRAYS, 4, STRIP, 128), F32),
            pltpu.VMEM((32, 48, 128), F32),
            pltpu.VMEM((32, 48, 128), F32),
            pltpu.VMEM((32, 48, 128), F32),
            pltpu.VMEM((32, 48, 128), F32),
            pltpu.VMEM((32, 48, 128), F32),
            pltpu.VMEM((512, STEPS, 128), F32),
            pltpu.VMEM((2, 2, MAIN, 128), F32),
            pltpu.VMEM((STEPS, 128), F32),
            pltpu.VMEM((STEPS, 128), F32),
            pltpu.VMEM((32, STEPS, 128), F32),
            dma((5,)),
            dma((ARRAYS, 2)), dma((ARRAYS, 2)),
            dma((ARRAYS, 2)), dma((ARRAYS, 2)),
            dma((ARRAYS, 8)), dma((ARRAYS, 8)),
            dma((2, 2)), dma((2, 2)),
            dma, dma, dma, dma, dma, dma((ARRAYS, 2, 2)), dma((ARRAYS, 2, 2)),
        ],
        compiler_params=pltpu.CompilerParams(
            collective_id=0, has_side_effects=True, vmem_limit_bytes=60 << 20
        ),
        name="fdtd",
    )(pressure_new, pressure_old, codes, loss_table, receivers)
    return pl.pallas_call(
        hand_over,
        out_shape=shapes,
        in_specs=[vmem] * 2,
        out_specs=(vmem,) * 3,
        name="hand_over",
    )(*results)


def solution(mesh):
    in_specs = (P("gx", "gy", "gz"), P("gx", "gy", "gz"), P("gx", "gy", "gz"), P(), P())
    out_specs = (P("gx", "gy", "gz"), P("gx", "gy", "gz"), P())
    return jax.shard_map(
        on_device, mesh=mesh, in_specs=in_specs, out_specs=out_specs, check_vma=False
    )
```

```python
import jax
import jax.numpy as jnp
from jax import lax
from jax.experimental import pallas as pl
from jax.experimental.pallas import tpu as pltpu
from jax.sharding import PartitionSpec as P

STEPS = 8
EDGE_PARAM = 0.1292
CORNER_PARAM = 0.0036
COURANT_SQUARED = 0.64
FACE_WEIGHT = COURANT_SQUARED * (1.0 - 4.0 * EDGE_PARAM + 4.0 * CORNER_PARAM)
EDGE_WEIGHT = COURANT_SQUARED * (EDGE_PARAM - 2.0 * CORNER_PARAM)
CORNER_WEIGHT = COURANT_SQUARED * CORNER_PARAM
CENTRE_WEIGHT = 2.0 * (
    1.0
    - 3.0 * COURANT_SQUARED
    + 6.0 * COURANT_SQUARED * EDGE_PARAM
    - 4.0 * COURANT_SQUARED * CORNER_PARAM
)

CENTRE_SCALED = CENTRE_WEIGHT / EDGE_WEIGHT
FACE_SCALED = FACE_WEIGHT / EDGE_WEIGHT
CORNER_SCALED = CORNER_WEIGHT / EDGE_WEIGHT

MESH = pl.DeviceIdType.MESH
F32 = jnp.float32
UNROLL = 16
ARRAYS = 3
MAIN = 128
STRIP = 16
LOW, HIGH = 8, 24
TOP, BOTTOM = 8, 40


def add_up(terms):
    while len(terms) > 1:
        terms = [sum(terms[i : i + 2]) for i in range(0, len(terms), 2)]
    return terms[0]


def kernel(
    new_hbm, old_hbm, codes_hbm, table_hbm, rec_hbm,
    outr, ztr,
    new_ref, old_ref, codes_ref, table_ref, rec_ref, places, turns,
    damp, snd, sndo, rcv, rcvo, reg_d, reg_old, reg_new, inv, dm, hist,
    outs, part, zsum, ptr,
    s_load, s_in, r_in, s_out, r_out, s_halo, r_halo, s_back, r_back, s_tz, r_tz, s_tp, r_tp, s_own, s_pass, r_pass,
):
    gx, gy, k = (lax.axis_index(a) for a in ("gx", "gy", "gz"))
    y, h = lax.div(gx, 2), lax.rem(gx, 2)
    z = h * 8 + k

    def at_z(place):
        place = lax.rem(place, 16)
        return (2 * y + lax.div(place, 8), gy, lax.rem(place, 8))

    def turned(place, by, size):
        place = place + by
        return jnp.where(place >= size, place - size, place)

    y_of = [2 * turned(y, i, 4) + h for i in range(4)]
    gy_of = [turned(gy, i, 8) for i in range(8)]
    plane = [(y_of[i], gy_of[j], k) for i in range(4) for j in range(8)]
    ring = []
    for i in range(16):
        place = turned(z, i, 16)
        upper = place >= 8
        ring.append(
            (2 * y + jnp.where(upper, 1, 0), gy, jnp.where(upper, place - 8, place))
        )
    plane_order = [i * 8 + j for i in (2, 1, 3, 0) for j in (4, 3, 5, 2, 6, 1, 7, 0)][:-1]
    ring_order = [8, 7, 9, 6, 10, 5, 11, 4, 12, 3, 13, 2, 14, 1, 15]

    regs = (reg_d, reg_old, reg_new)

    loads = [
        pltpu.make_async_copy(source, target, s_load.at[n])
        for n, (source, target) in enumerate(
            (
                (codes_hbm, codes_ref),
                (table_hbm, table_ref),
                (old_hbm, old_ref),
                (new_hbm, new_ref),
                (rec_hbm, rec_ref),
            )
        )
    ]

    barrier = pltpu.get_barrier_semaphore()
    for i in (4, 12, 5, 11, 3, 13, 2, 14):
        pl.semaphore_signal(barrier, 1, device_id=at_z(z + i), device_id_type=MESH)

    for i in plane_order:
        pl.semaphore_signal(barrier, 1, device_id=plane[i], device_id_type=MESH)

    for load in loads:
        load.start()

    role = jnp.where((z >= 4) & (z < 12), 0, 1)
    kk = jnp.where(role == 0, z - 4, lax.rem(z + 4, 16))
    has_outer = jnp.where(role == 0, kk > 0, kk < 7)
    inner_at = 64 - 8 * role
    outer_at = 120 * (1 - role)

    lane = lax.broadcasted_iota(jnp.int32, (32, 128), 1)
    low_lanes = lane < 64
    slot = lax.broadcasted_iota(jnp.int32, (STRIP, 128), 1) // 8

    def look_up(p, carry):
        codes = codes_ref[p]
        value = jnp.zeros((32, 128), F32)
        for material in range(16):
            value = jnp.where(codes == material, table_ref[material], value)
        damp[p] = value
        return carry

    loads[0].wait()
    loads[1].wait()
    for p in range(8):
        look_up(p, 0)

    def pack(a, ref):
        def pack_main(p, carry):
            first, second = ref[p], pltpu.roll(ref[p + 4], 64, 1)
            rows = pl.ds(p * 32, 32)
            snd[a, 0, rows, :] = jnp.where(low_lanes, first, second)
            snd[a, 1, rows, :] = jnp.where(low_lanes, second, first)
            return carry

        for p in range(4):
            pack_main(p, 0)
        strips = [jnp.zeros((STRIP, 128), F32)] * 4
        for p in range(8):
            value = ref[p]
            for n, begin in enumerate((64, 56, 120, 0)):
                upper = pltpu.roll(value[:16], (8 * p + 128 - begin) % 128, 1)
                lower = pltpu.roll(value[16:], (8 * p + 192 - begin) % 128, 1)
                strips[n] = jnp.where(slot == p, upper, strips[n])
                strips[n] = jnp.where(slot == p + 8, lower, strips[n])
        snd[a, 0, MAIN : MAIN + STRIP, :] = strips[0]
        snd[a, 1, MAIN : MAIN + STRIP, :] = strips[1]
        sndo[a, 0] = strips[2]
        sndo[a, 1] = strips[3]

    targets = (at_z(k + 4), at_z(k + 12))

    def to_middle(a, half):
        return pltpu.make_async_remote_copy(
            src_ref=snd.at[a, half],
            dst_ref=rcv.at[a, h],
            send_sem=s_in.at[a, half],
            recv_sem=r_in.at[a, h],
            device_id=targets[half],
            device_id_type=MESH,
        )

    def in_middle(a, source):
        return pltpu.make_async_remote_copy(
            src_ref=snd.at[a, 0],
            dst_ref=rcv.at[a, source],
            send_sem=s_in.at[a, 0],
            recv_sem=r_in.at[a, source],
            device_id=targets[0],
            device_id_type=MESH,
        )

    def outer(a, way, source):
        return pltpu.make_async_remote_copy(
            src_ref=sndo.at[a, way],
            dst_ref=rcvo.at[a, source],
            send_sem=s_out.at[a, way],
            recv_sem=r_out.at[a, source],
            device_id=at_z(k + 5) if way == 0 else at_z(k + 11),
            device_id_type=MESH,
        )

    outer_ways = (k < 7, k > 0)
    for a, ref in enumerate((damp, old_ref, new_ref)):
        if a:
            loads[a + 1].wait()
        pack(a, ref)
        if a == 0:
            pl.semaphore_wait(barrier, 39)
        if a == 2:
            for half in range(2):
                to_middle(0, half).wait_send()
        for way in range(2):

            @pl.when(outer_ways[way])
            def _(a=a, way=way):
                outer(a, way, h).start()

        for half in range(2):
            to_middle(a, half).start()

    def clear(ref, planes, rows):
        count = planes.stop - planes.start
        height = rows.stop - rows.start
        zeros = jnp.zeros((height, 128), F32)

        def one(p, carry):
            ref[planes.start + p, rows, :] = zeros
            return carry

        lax.fori_loop(0, count, one, 0)

    def clear_outside(refs):
        for here_, planes, rows in (
            (y == 0, slice(0, 8), slice(0, 48)),
            (y == 3, slice(24, 32), slice(0, 48)),
            (gy == 0, slice(0, 32), slice(0, 8)),
            (gy == 7, slice(0, 32), slice(40, 48)),
        ):

            @pl.when(here_)
            def _(planes=planes, rows=rows):
                for ref in refs:
                    clear(ref, planes, rows)

    clear_outside((reg_old, reg_new))

    loads[4].wait()

    def locate(r, carry):
        x_at = rec_ref[0, r] - y * 16
        y_at = rec_ref[1, r] - gy * 32
        z_at = rec_ref[2, r] - kk * 128
        inside = (x_at >= 0) & (x_at < 16) & (y_at >= 0) & (y_at < 32)
        inside &= (z_at >= role * 64) & (z_at < role * 64 + 64)
        places[r] = jnp.where(inside, x_at * 32 + y_at, 0)
        turns[r] = jnp.where(inside, lax.rem(r - z_at + 128, 128), -1)
        return carry

    lax.fori_loop(0, 128, locate, 0)

    main_lanes = lane // 64 == role
    inner_lanes = (lane >= inner_at) & (lane < inner_at + 8)
    outer_lanes = (lane >= outer_at) & (
        lane < outer_at + jnp.where(has_outer, 8, 0)
    )
    some_lanes = main_lanes | inner_lanes | outer_lanes

    plane_of = (8, 16, 0, 24)

    def unpack(a, source):
        inner_strip = rcv[a, source, MAIN : MAIN + STRIP, :]
        outer_strip = rcvo[a, source]

        def spread(strip, p, begin):
            upper = pltpu.roll(strip, lax.rem(begin + 128 - 8 * p, 128), 1)
            lower = pltpu.roll(strip, lax.rem(begin + 192 - 8 * p, 128), 1)
            return jnp.concatenate([upper, lower], axis=0)

        def one(p, carry):
            packed = rcv[a, source, pl.ds(p * 32, 32), :]
            for q, main in ((p, packed), (p + 4, pltpu.roll(packed, 64, 1))):
                value = jnp.where(main_lanes, main, 0.0)
                value = jnp.where(inner_lanes, spread(inner_strip, q, inner_at), value)
                value = jnp.where(outer_lanes, spread(outer_strip, q, outer_at), value)
                regs[a][plane_of[source] + q, TOP:BOTTOM, :] = value
            return carry

        for p in range(4):
            one(p, 0)

    ways = [(-1, -1), (-1, 1), (1, -1), (1, 1), (0, -1), (0, 1)]
    x_from = {-1: (8, 8), 0: (8, 16), 1: (16, 8)}
    x_to = {-1: (24, 8), 0: (8, 16), 1: (0, 8)}
    y_from = {-1: (8, 8), 0: (8, 32), 1: (32, 8)}
    y_to = {-1: (40, 8), 0: (8, 32), 1: (0, 8)}
    there_x = {-1: y > 0, 0: None, 1: y < 3}
    there_y = {-1: gy > 0, 0: None, 1: gy < 7}

    def exists(i, j):
        if there_x[i] is None:
            return there_y[j]
        if there_y[j] is None:
            return there_x[i]
        return there_x[i] & there_y[j]

    def halo(a, n):
        i, j = ways[n]
        (xf, xn), (yf, yn) = x_from[i], y_from[j]
        (xt, _), (yt, _) = x_to[i], y_to[j]
        return pltpu.make_async_remote_copy(
            src_ref=regs[a].at[pl.ds(xf, xn), pl.ds(yf, yn), :],
            dst_ref=regs[a].at[pl.ds(xt, xn), pl.ds(yt, yn), :],
            send_sem=s_halo.at[a, n],
            recv_sem=r_halo.at[a, n],
            device_id=(gx + 2 * i, gy + j, k),
            device_id_type=MESH,
        )

    def pass_on(a, source):
        i = 2 * source - 1
        copies = []
        for n, ref in enumerate((rcv, rcvo)):
            copies.append(
                pltpu.make_async_remote_copy(
                    src_ref=ref.at[a, source],
                    dst_ref=ref.at[a, 3 - source],
                    send_sem=s_pass.at[a, source, n],
                    recv_sem=r_pass.at[a, 3 - source - 2, n],
                    device_id=(gx + 2 * i, gy, k),
                    device_id_type=MESH,
                )
            )
        return copies

    def each_pass(a, source, there, act):
        block, strip = pass_on(a, source)

        @pl.when(there & has_outer)
        def _():
            act(strip)

        @pl.when(there)
        def _():
            act(block)

    def send_pass(a, source):
        each_pass(a, source, y < 3 if source else y > 0, lambda copy: copy.start())

    def left_pass(a, source):
        each_pass(a, source, y < 3 if source else y > 0, lambda copy: copy.wait_send())

    def wait_pass(a, source):
        there = y > 0 if source else y < 3
        each_pass(a, source, there, lambda copy: copy.wait_recv())

        @pl.when(there)
        def _():
            unpack(a, 3 - source)

    def send_halos(a):
        for n, way in enumerate(ways):

            @pl.when(exists(*way))
            def _(n=n):
                halo(a, n).start()

    def left_halos(a):
        for n, way in enumerate(ways):

            @pl.when(exists(*way))
            def _(n=n):
                halo(a, n).wait_send()

    def wait_halos(a):
        for n, (i, j) in enumerate(ways):

            @pl.when(exists(-i, -j))
            def _(n=n):
                halo(a, n).wait_recv()

    def take_halos(a):
        for source in range(2):
            wait_pass(a, source)
        wait_halos(a)

    def coefficients():
        lanes = jnp.concatenate([some_lanes, some_lanes[:16]], axis=0)

        def one(p, carry):
            d = reg_d[p]
            scale = jnp.where(lanes, 1.0 / (1.0 + d), 0.0)
            inv[p] = EDGE_WEIGHT * scale
            dm[p] = jnp.where(lanes, (d - 1.0) * scale, 0.0)
            return carry

        def four(n, carry):
            for u in range(4):
                one(n * 4 + u, carry)
            return carry

        lax.fori_loop(0, 8, four, 0)
        clear_outside((inv, dm))

    for a in range(ARRAYS):
        for source in range(2):

            @pl.when(has_outer)
            def _(a=a, source=source):
                outer(a, 0, source).wait_recv()

            in_middle(a, source).wait_recv()
            send_pass(a, source)
        for source in range(2):
            unpack(a, source)
        send_halos(a)
        if a == 1:
            take_halos(0)
            coefficients()
    take_halos(1)
    take_halos(2)
    left_halos(1)

    def to_home(level, source):
        return pltpu.make_async_remote_copy(
            src_ref=outs.at[level, source],
            dst_ref=outr.at[level, role],
            send_sem=s_back.at[level, source],
            recv_sem=r_back.at[level, role],
            device_id=at_z(kk + 8 * source),
            device_id_type=MESH,
        )

    def at_home(level, half):
        return pltpu.make_async_remote_copy(
            src_ref=outs.at[level, 0],
            dst_ref=outr.at[level, half],
            send_sem=s_back.at[level, 0],
            recv_sem=r_back.at[level, half],
            device_id=at_z(kk),
            device_id_type=MESH,
        )

    def send_back(level, field):
        for source in range(2):

            def pack_back(p, carry, source=source):
                first = field[LOW + source * 8 + p, TOP:BOTTOM, :]
                second = field[LOW + source * 8 + 4 + p, TOP:BOTTOM, :]
                outs[level, source, pl.ds(p * 32, 32), :] = (
                    jnp.where(main_lanes, first, pltpu.roll(second, 64, 1))
                )
                return carry

            for p in range(4):
                pack_back(p, 0)
            to_home(level, source).start()

    def spread_plane(v):
        side = pltpu.roll(v, 1, 1) + pltpu.roll(v, 127, 1)
        return (
            CENTRE_SCALED * v + FACE_SCALED * side,
            FACE_SCALED * v + side,
            v + CORNER_SCALED * side,
        )

    for step in range(1, STEPS + 1):
        cur, prev = (reg_new, reg_old) if step % 2 else (reg_old, reg_new)

        def one(p, carry, cur=cur, prev=prev):
            total, rows, b, c = carry
            a_next, b_next, c_next = spread_plane(cur[p + 1])
            rows = rows + c_next
            total = total + b_next + (pltpu.roll(rows, 1, 0) + pltpu.roll(rows, 47, 0))
            prev[p] = total * inv[p] + dm[p] * prev[p]
            return a_next + b, b_next + c, b_next, c_next

        def several(n, carry, one=one, step=step):
            for u in range(UNROLL):
                carry = one(step + n * UNROLL + u, carry)
            return carry

        if step == 2:
            left_halos(2)
        _, b, c = spread_plane(cur[step - 1])
        a_next, b_next, c_next = spread_plane(cur[step])
        carry = (a_next + b, b_next + c, b_next, c_next)
        loops, rest = divmod(32 - 2 * step, UNROLL)
        carry = lax.fori_loop(0, loops, several, carry)
        for p in range(32 - step - rest, 32 - step):
            carry = one(p, carry)

        if step >= STEPS - 1:
            send_back(step - STEPS + 1, prev)

        def keep(p, carry, prev=prev, step=step):
            rows = pl.ds(p * 256 + step - 1, 32, stride=8)
            hist.reshape(512 * STEPS, 128)[rows, :] = prev[LOW + p, TOP:BOTTOM, :]
            return carry

        for p in range(16):
            keep(p, 0)

    lanes8 = lax.broadcasted_iota(jnp.int32, (STEPS, 128), 1)

    def sample(n, picked):
        for u in range(8):
            r = n * 8 + u
            turn = turns[r]
            rows = pltpu.roll(hist[places[r]], jnp.maximum(turn, 0), 1)
            picked = jnp.where(lanes8 == jnp.where(turn >= 0, r, -1), rows, picked)
        return picked

    part[...] = lax.fori_loop(0, 16, sample, jnp.zeros((STEPS, 128), F32))

    def in_plane(i):
        return pltpu.make_async_remote_copy(
            src_ref=part,
            dst_ref=ptr.at[i],
            send_sem=s_tp,
            recv_sem=r_tp,
            device_id=plane[i],
            device_id_type=MESH,
        )

    def in_ring(i):
        return pltpu.make_async_remote_copy(
            src_ref=zsum,
            dst_ref=ztr.at[i],
            send_sem=s_tz,
            recv_sem=r_tz,
            device_id=ring[i],
            device_id_type=MESH,
        )

    def whole(slots, send_sem, recv_sem, target):
        others = slots.at[pl.ds(1, slots.shape[0] - 1)]
        return pltpu.make_async_remote_copy(
            src_ref=others,
            dst_ref=others,
            send_sem=send_sem,
            recv_sem=recv_sem,
            device_id=target,
            device_id_type=MESH,
        )

    all_plane = whole(ptr, s_tp, r_tp, plane[1])
    all_ring = whole(ztr, s_tz, r_tz, ring[1])
    for i in plane_order:
        in_plane(i).start()
    all_plane.wait_recv()
    zsum[...] = add_up([part[...]] + [ptr[i] for i in range(1, 32)])
    own = pltpu.make_async_copy(zsum, ztr.at[0], s_own)
    own.start()
    for i in ring_order:
        in_ring(i).start()

    for level in range(2):
        for half in range(2):
            at_home(level, half).wait_recv()
    all_ring.wait_recv()
    own.wait()

    for a in range(ARRAYS):
        for half in range(2):
            if a > 0:
                to_middle(a, half).wait_send()
        for way in range(2):

            @pl.when(outer_ways[way])
            def _(a=a, way=way):
                outer(a, way, h).wait_send()

    left_halos(0)
    for a in range(ARRAYS):
        for source in range(2):
            left_pass(a, source)

    for level in range(2):
        for source in range(2):
            to_home(level, source).wait_send()

    all_plane.wait_send()
    all_ring.wait_send()


def hand_over(packed, sums, new, old, traces):
    low_lanes = lax.broadcasted_iota(jnp.int32, (32, 128), 1) < 64
    for level, ref in ((0, old), (1, new)):
        for p in range(4):
            rows = slice(p * 32, (p + 1) * 32)
            left, right = packed[level, 0, rows, :], packed[level, 1, rows, :]
            ref[p] = jnp.where(low_lanes, left, right)
            ref[p + 4] = pltpu.roll(jnp.where(low_lanes, right, left), 64, 1)
    traces[...] = add_up([sums[i] for i in range(16)])


def on_device(pressure_new, pressure_old, codes, loss_table, receivers):
    vmem = pl.BlockSpec(memory_space=pltpu.VMEM)
    anywhere = pl.BlockSpec(memory_space=pl.ANY)
    block = jax.ShapeDtypeStruct((8, 32, 128), F32)
    dma = pltpu.SemaphoreType.DMA
    shapes = (block, block, jax.ShapeDtypeStruct((STEPS, 128), F32))
    results = pl.pallas_call(
        kernel,
        out_shape=(
            jax.ShapeDtypeStruct((2, 2, MAIN, 128), F32),
            jax.ShapeDtypeStruct((16, STEPS, 128), F32),
        ),
        in_specs=[anywhere] * 5,
        out_specs=(anywhere, anywhere),
        scratch_shapes=[
            pltpu.VMEM((8, 32, 128), F32),
            pltpu.VMEM((8, 32, 128), F32),
            pltpu.VMEM((8, 32, 128), jnp.int32),
            pltpu.SMEM((16,), F32),
            pltpu.SMEM((3, 128), jnp.int32),
            pltpu.SMEM((128,), jnp.int32),
            pltpu.SMEM((128,), jnp.int32),
            pltpu.VMEM((8, 32, 128), F32),
            pltpu.VMEM((ARRAYS, 2, MAIN + STRIP, 128), F32),
            pltpu.VMEM((ARRAYS, 2, STRIP, 128), F32),
            pltpu.VMEM((ARRAYS, 4, MAIN + STRIP, 128), F32),
            pltpu.VMEM((ARRAYS, 4, STRIP, 128), F32),
            pltpu.VMEM((32, 48, 128), F32),
            pltpu.VMEM((32, 48, 128), F32),
            pltpu.VMEM((32, 48, 128), F32),
            pltpu.VMEM((32, 48, 128), F32),
            pltpu.VMEM((32, 48, 128), F32),
            pltpu.VMEM((512, STEPS, 128), F32),
            pltpu.VMEM((2, 2, MAIN, 128), F32),
            pltpu.VMEM((STEPS, 128), F32),
            pltpu.VMEM((STEPS, 128), F32),
            pltpu.VMEM((32, STEPS, 128), F32),
            dma((5,)),
            dma((ARRAYS, 2)), dma((ARRAYS, 2)),
            dma((ARRAYS, 2)), dma((ARRAYS, 2)),
            dma((ARRAYS, 8)), dma((ARRAYS, 8)),
            dma((2, 2)), dma((2, 2)),
            dma, dma, dma, dma, dma, dma((ARRAYS, 2, 2)), dma((ARRAYS, 2, 2)),
        ],
        compiler_params=pltpu.CompilerParams(
            collective_id=0, has_side_effects=True, vmem_limit_bytes=60 << 20
        ),
        name="fdtd",
    )(pressure_new, pressure_old, codes, loss_table, receivers)
    return pl.pallas_call(
        hand_over,
        out_shape=shapes,
        in_specs=[vmem] * 2,
        out_specs=(vmem,) * 3,
        name="hand_over",
    )(*results)


def solution(mesh):
    in_specs = (P("gx", "gy", "gz"), P("gx", "gy", "gz"), P("gx", "gy", "gz"), P(), P())
    out_specs = (P("gx", "gy", "gz"), P("gx", "gy", "gz"), P())
    return jax.shard_map(
        on_device, mesh=mesh, in_specs=in_specs, out_specs=out_specs, check_vma=False
    )
```

```python
import jax
import jax.numpy as jnp
from jax import lax
from jax.experimental import pallas as pl
from jax.experimental.pallas import tpu as pltpu
from jax.sharding import PartitionSpec as P

STEPS = 8
EDGE_PARAM = 0.1292
CORNER_PARAM = 0.0036
COURANT_SQUARED = 0.64
FACE_WEIGHT = COURANT_SQUARED * (1.0 - 4.0 * EDGE_PARAM + 4.0 * CORNER_PARAM)
EDGE_WEIGHT = COURANT_SQUARED * (EDGE_PARAM - 2.0 * CORNER_PARAM)
CORNER_WEIGHT = COURANT_SQUARED * CORNER_PARAM
CENTRE_WEIGHT = 2.0 * (
    1.0
    - 3.0 * COURANT_SQUARED
    + 6.0 * COURANT_SQUARED * EDGE_PARAM
    - 4.0 * COURANT_SQUARED * CORNER_PARAM
)

CENTRE_SCALED = CENTRE_WEIGHT / EDGE_WEIGHT
FACE_SCALED = FACE_WEIGHT / EDGE_WEIGHT
CORNER_SCALED = CORNER_WEIGHT / EDGE_WEIGHT

MESH = pl.DeviceIdType.MESH
F32 = jnp.float32
UNROLL = 16
ARRAYS = 3
MAIN = 128
STRIP = 16
LOW, HIGH = 8, 24
TOP, BOTTOM = 8, 40


def add_up(terms):
    while len(terms) > 1:
        terms = [sum(terms[i : i + 2]) for i in range(0, len(terms), 2)]
    return terms[0]


def kernel(
    new_hbm, old_hbm, codes_hbm, table_hbm, rec_hbm,
    outr, ztr,
    new_ref, old_ref, codes_ref, table_ref, rec_ref, places, turns,
    damp, snd, sndo, rcv, rcvo, reg_d, reg_old, reg_new, inv, dm, hist,
    outs, part, zsum, ptr,
    s_load, s_in, r_in, s_out, r_out, s_halo, r_halo, s_back, r_back, s_tz, r_tz, s_tp, r_tp, s_own, s_pass, r_pass,
):
    gx, gy, k = (lax.axis_index(a) for a in ("gx", "gy", "gz"))
    y, h = lax.div(gx, 2), lax.rem(gx, 2)
    z = h * 8 + k

    def at_z(place):
        place = lax.rem(place, 16)
        return (2 * y + lax.div(place, 8), gy, lax.rem(place, 8))

    def turned(place, by, size):
        place = place + by
        return jnp.where(place >= size, place - size, place)

    y_of = [2 * turned(y, i, 4) + h for i in range(4)]
    gy_of = [turned(gy, i, 8) for i in range(8)]
    plane = [(y_of[i], gy_of[j], k) for i in range(4) for j in range(8)]
    ring = []
    for i in range(16):
        place = turned(z, i, 16)
        upper = place >= 8
        ring.append(
            (2 * y + jnp.where(upper, 1, 0), gy, jnp.where(upper, place - 8, place))
        )
    plane_order = [i * 8 + j for i in (2, 1, 3, 0) for j in (4, 3, 5, 2, 6, 1, 7, 0)][:-1]
    ring_order = [8, 7, 9, 6, 10, 5, 11, 4, 12, 3, 13, 2, 14, 1, 15]

    regs = (reg_d, reg_old, reg_new)

    loads = [
        pltpu.make_async_copy(source, target, s_load.at[n])
        for n, (source, target) in enumerate(
            (
                (codes_hbm, codes_ref),
                (table_hbm, table_ref),
                (old_hbm, old_ref),
                (new_hbm, new_ref),
                (rec_hbm, rec_ref),
            )
        )
    ]

    barrier = pltpu.get_barrier_semaphore()
    for i in (4, 12, 5, 11, 3, 13, 2, 14):
        pl.semaphore_signal(barrier, 1, device_id=at_z(z + i), device_id_type=MESH)

    for i in plane_order:
        pl.semaphore_signal(barrier, 1, device_id=plane[i], device_id_type=MESH)

    for load in loads:
        load.start()

    role = jnp.where((z >= 4) & (z < 12), 0, 1)
    kk = jnp.where(role == 0, z - 4, lax.rem(z + 4, 16))
    has_outer = jnp.where(role == 0, kk > 0, kk < 7)
    inner_at = 64 - 8 * role
    outer_at = 120 * (1 - role)

    lane = lax.broadcasted_iota(jnp.int32, (32, 128), 1)
    low_lanes = lane < 64
    slot = lax.broadcasted_iota(jnp.int32, (STRIP, 128), 1) // 8

    def look_up(p, carry):
        codes = codes_ref[p]
        value = jnp.zeros((32, 128), F32)
        for material in range(16):
            value = jnp.where(codes == material, table_ref[material], value)
        damp[p] = value
        return carry

    loads[0].wait()
    loads[1].wait()
    for p in range(8):
        look_up(p, 0)

    def pack(a, ref):
        def pack_main(p, carry):
            first, second = ref[p], pltpu.roll(ref[p + 4], 64, 1)
            rows = pl.ds(p * 32, 32)
            snd[a, 0, rows, :] = jnp.where(low_lanes, first, second)
            snd[a, 1, rows, :] = jnp.where(low_lanes, second, first)
            return carry

        for p in range(4):
            pack_main(p, 0)
        strips = [jnp.zeros((STRIP, 128), F32)] * 4
        for p in range(8):
            value = ref[p]
            for n, begin in enumerate((64, 56, 120, 0)):
                upper = pltpu.roll(value[:16], (8 * p + 128 - begin) % 128, 1)
                lower = pltpu.roll(value[16:], (8 * p + 192 - begin) % 128, 1)
                strips[n] = jnp.where(slot == p, upper, strips[n])
                strips[n] = jnp.where(slot == p + 8, lower, strips[n])
        snd[a, 0, MAIN : MAIN + STRIP, :] = strips[0]
        snd[a, 1, MAIN : MAIN + STRIP, :] = strips[1]
        sndo[a, 0] = strips[2]
        sndo[a, 1] = strips[3]

    targets = (at_z(k + 4), at_z(k + 12))

    def to_middle(a, half):
        return pltpu.make_async_remote_copy(
            src_ref=snd.at[a, half],
            dst_ref=rcv.at[a, h],
            send_sem=s_in.at[a, half],
            recv_sem=r_in.at[a, h],
            device_id=targets[half],
            device_id_type=MESH,
        )

    def in_middle(a, source):
        return pltpu.make_async_remote_copy(
            src_ref=snd.at[a, 0],
            dst_ref=rcv.at[a, source],
            send_sem=s_in.at[a, 0],
            recv_sem=r_in.at[a, source],
            device_id=targets[0],
            device_id_type=MESH,
        )

    def outer(a, way, source):
        return pltpu.make_async_remote_copy(
            src_ref=sndo.at[a, way],
            dst_ref=rcvo.at[a, source],
            send_sem=s_out.at[a, way],
            recv_sem=r_out.at[a, source],
            device_id=at_z(k + 5) if way == 0 else at_z(k + 11),
            device_id_type=MESH,
        )

    outer_ways = (k < 7, k > 0)
    for a, ref in enumerate((damp, old_ref, new_ref)):
        if a:
            loads[a + 1].wait()
        pack(a, ref)
        if a == 0:
            pl.semaphore_wait(barrier, 39)
        if a == 2:
            for half in range(2):
                to_middle(0, half).wait_send()
        for way in range(2):

            @pl.when(outer_ways[way])
            def _(a=a, way=way):
                outer(a, way, h).start()

        for half in range(2):
            to_middle(a, half).start()

    def clear(ref, planes, rows):
        count = planes.stop - planes.start
        height = rows.stop - rows.start
        zeros = jnp.zeros((height, 128), F32)

        def one(p, carry):
            ref[planes.start + p, rows, :] = zeros
            return carry

        lax.fori_loop(0, count, one, 0)

    def clear_outside(refs):
        for here_, planes, rows in (
            (y == 0, slice(0, 8), slice(0, 48)),
            (y == 3, slice(24, 32), slice(0, 48)),
            (gy == 0, slice(0, 32), slice(0, 8)),
            (gy == 7, slice(0, 32), slice(40, 48)),
        ):

            @pl.when(here_)
            def _(planes=planes, rows=rows):
                for ref in refs:
                    clear(ref, planes, rows)

    clear_outside((reg_old, reg_new))

    loads[4].wait()

    def locate(r, carry):
        x_at = rec_ref[0, r] - y * 16
        y_at = rec_ref[1, r] - gy * 32
        z_at = rec_ref[2, r] - kk * 128
        inside = (x_at >= 0) & (x_at < 16) & (y_at >= 0) & (y_at < 32)
        inside &= (z_at >= role * 64) & (z_at < role * 64 + 64)
        places[r] = jnp.where(inside, x_at * 32 + y_at, 0)
        turns[r] = jnp.where(inside, lax.rem(r - z_at + 128, 128), -1)
        return carry

    lax.fori_loop(0, 128, locate, 0)

    main_lanes = lane // 64 == role
    inner_lanes = (lane >= inner_at) & (lane < inner_at + 8)
    outer_lanes = (lane >= outer_at) & (
        lane < outer_at + jnp.where(has_outer, 8, 0)
    )
    some_lanes = main_lanes | inner_lanes | outer_lanes

    plane_of = (8, 16, 0, 24)

    def unpack(a, source):
        inner_strip = rcv[a, source, MAIN : MAIN + STRIP, :]
        outer_strip = rcvo[a, source]

        def spread(strip, p, begin):
            upper = pltpu.roll(strip, lax.rem(begin + 128 - 8 * p, 128), 1)
            lower = pltpu.roll(strip, lax.rem(begin + 192 - 8 * p, 128), 1)
            return jnp.concatenate([upper, lower], axis=0)

        def one(p, carry):
            packed = rcv[a, source, pl.ds(p * 32, 32), :]
            for q, main in ((p, packed), (p + 4, pltpu.roll(packed, 64, 1))):
                value = jnp.where(main_lanes, main, 0.0)
                value = jnp.where(inner_lanes, spread(inner_strip, q, inner_at), value)
                value = jnp.where(outer_lanes, spread(outer_strip, q, outer_at), value)
                regs[a][plane_of[source] + q, TOP:BOTTOM, :] = value
            return carry

        for p in range(4):
            one(p, 0)

    ways = [(-1, -1), (-1, 1), (1, -1), (1, 1), (0, -1), (0, 1)]
    x_from = {-1: (8, 8), 0: (8, 16), 1: (16, 8)}
    x_to = {-1: (24, 8), 0: (8, 16), 1: (0, 8)}
    y_from = {-1: (8, 8), 0: (8, 32), 1: (32, 8)}
    y_to = {-1: (40, 8), 0: (8, 32), 1: (0, 8)}
    there_x = {-1: y > 0, 0: None, 1: y < 3}
    there_y = {-1: gy > 0, 0: None, 1: gy < 7}

    def exists(i, j):
        if there_x[i] is None:
            return there_y[j]
        if there_y[j] is None:
            return there_x[i]
        return there_x[i] & there_y[j]

    def halo(a, n):
        i, j = ways[n]
        (xf, xn), (yf, yn) = x_from[i], y_from[j]
        (xt, _), (yt, _) = x_to[i], y_to[j]
        return pltpu.make_async_remote_copy(
            src_ref=regs[a].at[pl.ds(xf, xn), pl.ds(yf, yn), :],
            dst_ref=regs[a].at[pl.ds(xt, xn), pl.ds(yt, yn), :],
            send_sem=s_halo.at[a, n],
            recv_sem=r_halo.at[a, n],
            device_id=(gx + 2 * i, gy + j, k),
            device_id_type=MESH,
        )

    def pass_on(a, source):
        i = 2 * source - 1
        copies = []
        for n, ref in enumerate((rcv, rcvo)):
            copies.append(
                pltpu.make_async_remote_copy(
                    src_ref=ref.at[a, source],
                    dst_ref=ref.at[a, 3 - source],
                    send_sem=s_pass.at[a, source, n],
                    recv_sem=r_pass.at[a, 3 - source - 2, n],
                    device_id=(gx + 2 * i, gy, k),
                    device_id_type=MESH,
                )
            )
        return copies

    def each_pass(a, source, there, act):
        block, strip = pass_on(a, source)

        @pl.when(there & has_outer)
        def _():
            act(strip)

        @pl.when(there)
        def _():
            act(block)

    def send_pass(a, source):
        each_pass(a, source, y < 3 if source else y > 0, lambda copy: copy.start())

    def left_pass(a, source):
        each_pass(a, source, y < 3 if source else y > 0, lambda copy: copy.wait_send())

    def wait_pass(a, source):
        there = y > 0 if source else y < 3
        each_pass(a, source, there, lambda copy: copy.wait_recv())

        @pl.when(there)
        def _():
            unpack(a, 3 - source)

    def send_halos(a):
        for n, way in enumerate(ways):

            @pl.when(exists(*way))
            def _(n=n):
                halo(a, n).start()

    def left_halos(a):
        for n, way in enumerate(ways):

            @pl.when(exists(*way))
            def _(n=n):
                halo(a, n).wait_send()

    def wait_halos(a):
        for n, (i, j) in enumerate(ways):

            @pl.when(exists(-i, -j))
            def _(n=n):
                halo(a, n).wait_recv()

    def take_halos(a):
        for source in range(2):
            wait_pass(a, source)
        wait_halos(a)

    def coefficients():
        lanes = jnp.concatenate([some_lanes, some_lanes[:16]], axis=0)

        def one(p, carry):
            d = reg_d[p]
            scale = jnp.where(lanes, 1.0 / (1.0 + d), 0.0)
            inv[p] = EDGE_WEIGHT * scale
            dm[p] = jnp.where(lanes, (d - 1.0) * scale, 0.0)
            return carry

        def four(n, carry):
            for u in range(4):
                one(n * 4 + u, carry)
            return carry

        lax.fori_loop(0, 8, four, 0)
        clear_outside((inv, dm))

    for a in range(ARRAYS):
        for source in range(2):

            @pl.when(has_outer)
            def _(a=a, source=source):
                outer(a, 0, source).wait_recv()

            in_middle(a, source).wait_recv()
            send_pass(a, source)
        for source in range(2):
            unpack(a, source)
        send_halos(a)
        if a == 1:
            take_halos(0)
            coefficients()
    take_halos(1)
    take_halos(2)
    left_halos(1)

    def to_home(level, source):
        return pltpu.make_async_remote_copy(
            src_ref=outs.at[level, source],
            dst_ref=outr.at[level, role],
            send_sem=s_back.at[level, source],
            recv_sem=r_back.at[level, role],
            device_id=at_z(kk + 8 * source),
            device_id_type=MESH,
        )

    def at_home(level, half):
        return pltpu.make_async_remote_copy(
            src_ref=outs.at[level, 0],
            dst_ref=outr.at[level, half],
            send_sem=s_back.at[level, 0],
            recv_sem=r_back.at[level, half],
            device_id=at_z(kk),
            device_id_type=MESH,
        )

    def send_back(level, field):
        for source in range(2):

            def pack_back(p, carry, source=source):
                first = field[LOW + source * 8 + p, TOP:BOTTOM, :]
                second = field[LOW + source * 8 + 4 + p, TOP:BOTTOM, :]
                outs[level, source, pl.ds(p * 32, 32), :] = (
                    jnp.where(main_lanes, first, pltpu.roll(second, 64, 1))
                )
                return carry

            for p in range(4):
                pack_back(p, 0)
            to_home(level, source).start()

    def spread_plane(v):
        side = pltpu.roll(v, 1, 1) + pltpu.roll(v, 127, 1)
        return (
            CENTRE_SCALED * v + FACE_SCALED * side,
            FACE_SCALED * v + side,
            v + CORNER_SCALED * side,
        )

    for step in range(1, STEPS + 1):
        cur, prev = (reg_new, reg_old) if step % 2 else (reg_old, reg_new)

        def one(p, carry, cur=cur, prev=prev, step=step):
            total, rows, b, c = carry
            a_next, b_next, c_next = spread_plane(cur[p + 1])
            rows = rows + c_next
            total = total + b_next + (pltpu.roll(rows, 1, 0) + pltpu.roll(rows, 47, 0))
            own = slice(TOP, BOTTOM) if step == STEPS else slice(0, 48)
            prev[p, own, :] = total[own] * inv[p, own, :] + dm[p, own, :] * prev[p, own, :]
            return a_next + b, b_next + c, b_next, c_next

        def several(n, carry, one=one, step=step):
            for u in range(UNROLL):
                carry = one(step + n * UNROLL + u, carry)
            return carry

        if step == 2:
            left_halos(2)
        _, b, c = spread_plane(cur[step - 1])
        a_next, b_next, c_next = spread_plane(cur[step])
        carry = (a_next + b, b_next + c, b_next, c_next)
        loops, rest = divmod(32 - 2 * step, UNROLL)
        carry = lax.fori_loop(0, loops, several, carry)
        for p in range(32 - step - rest, 32 - step):
            carry = one(p, carry)

        if step >= STEPS - 1:
            send_back(step - STEPS + 1, prev)

        def keep(p, carry, prev=prev, step=step):
            rows = pl.ds(p * 256 + step - 1, 32, stride=8)
            hist.reshape(512 * STEPS, 128)[rows, :] = prev[LOW + p, TOP:BOTTOM, :]
            return carry

        for p in range(16):
            keep(p, 0)

    lanes8 = lax.broadcasted_iota(jnp.int32, (STEPS, 128), 1)

    def sample(n, picked):
        for u in range(8):
            r = n * 8 + u
            turn = turns[r]
            rows = pltpu.roll(hist[places[r]], jnp.maximum(turn, 0), 1)
            picked = jnp.where(lanes8 == jnp.where(turn >= 0, r, -1), rows, picked)
        return picked

    part[...] = lax.fori_loop(0, 16, sample, jnp.zeros((STEPS, 128), F32))

    def in_plane(i):
        return pltpu.make_async_remote_copy(
            src_ref=part,
            dst_ref=ptr.at[i],
            send_sem=s_tp,
            recv_sem=r_tp,
            device_id=plane[i],
            device_id_type=MESH,
        )

    def in_ring(i):
        return pltpu.make_async_remote_copy(
            src_ref=zsum,
            dst_ref=ztr.at[i],
            send_sem=s_tz,
            recv_sem=r_tz,
            device_id=ring[i],
            device_id_type=MESH,
        )

    def whole(slots, send_sem, recv_sem, target):
        others = slots.at[pl.ds(1, slots.shape[0] - 1)]
        return pltpu.make_async_remote_copy(
            src_ref=others,
            dst_ref=others,
            send_sem=send_sem,
            recv_sem=recv_sem,
            device_id=target,
            device_id_type=MESH,
        )

    all_plane = whole(ptr, s_tp, r_tp, plane[1])
    all_ring = whole(ztr, s_tz, r_tz, ring[1])
    for i in plane_order:
        in_plane(i).start()
    all_plane.wait_recv()
    zsum[...] = add_up([part[...]] + [ptr[i] for i in range(1, 32)])
    own = pltpu.make_async_copy(zsum, ztr.at[0], s_own)
    own.start()
    for i in ring_order:
        in_ring(i).start()

    for level in range(2):
        for half in range(2):
            at_home(level, half).wait_recv()
    all_ring.wait_recv()
    own.wait()

    for a in range(ARRAYS):
        for half in range(2):
            if a > 0:
                to_middle(a, half).wait_send()
        for way in range(2):

            @pl.when(outer_ways[way])
            def _(a=a, way=way):
                outer(a, way, h).wait_send()

    left_halos(0)
    for a in range(ARRAYS):
        for source in range(2):
            left_pass(a, source)

    for level in range(2):
        for source in range(2):
            to_home(level, source).wait_send()

    all_plane.wait_send()
    all_ring.wait_send()


def hand_over(packed, sums, new, old, traces):
    low_lanes = lax.broadcasted_iota(jnp.int32, (32, 128), 1) < 64
    for level, ref in ((0, old), (1, new)):
        for p in range(4):
            rows = slice(p * 32, (p + 1) * 32)
            left, right = packed[level, 0, rows, :], packed[level, 1, rows, :]
            ref[p] = jnp.where(low_lanes, left, right)
            ref[p + 4] = pltpu.roll(jnp.where(low_lanes, right, left), 64, 1)
    traces[...] = add_up([sums[i] for i in range(16)])


def on_device(pressure_new, pressure_old, codes, loss_table, receivers):
    vmem = pl.BlockSpec(memory_space=pltpu.VMEM)
    anywhere = pl.BlockSpec(memory_space=pl.ANY)
    block = jax.ShapeDtypeStruct((8, 32, 128), F32)
    dma = pltpu.SemaphoreType.DMA
    shapes = (block, block, jax.ShapeDtypeStruct((STEPS, 128), F32))
    results = pl.pallas_call(
        kernel,
        out_shape=(
            jax.ShapeDtypeStruct((2, 2, MAIN, 128), F32),
            jax.ShapeDtypeStruct((16, STEPS, 128), F32),
        ),
        in_specs=[anywhere] * 5,
        out_specs=(anywhere, anywhere),
        scratch_shapes=[
            pltpu.VMEM((8, 32, 128), F32),
            pltpu.VMEM((8, 32, 128), F32),
            pltpu.VMEM((8, 32, 128), jnp.int32),
            pltpu.SMEM((16,), F32),
            pltpu.SMEM((3, 128), jnp.int32),
            pltpu.SMEM((128,), jnp.int32),
            pltpu.SMEM((128,), jnp.int32),
            pltpu.VMEM((8, 32, 128), F32),
            pltpu.VMEM((ARRAYS, 2, MAIN + STRIP, 128), F32),
            pltpu.VMEM((ARRAYS, 2, STRIP, 128), F32),
            pltpu.VMEM((ARRAYS, 4, MAIN + STRIP, 128), F32),
            pltpu.VMEM((ARRAYS, 4, STRIP, 128), F32),
            pltpu.VMEM((32, 48, 128), F32),
            pltpu.VMEM((32, 48, 128), F32),
            pltpu.VMEM((32, 48, 128), F32),
            pltpu.VMEM((32, 48, 128), F32),
            pltpu.VMEM((32, 48, 128), F32),
            pltpu.VMEM((512, STEPS, 128), F32),
            pltpu.VMEM((2, 2, MAIN, 128), F32),
            pltpu.VMEM((STEPS, 128), F32),
            pltpu.VMEM((STEPS, 128), F32),
            pltpu.VMEM((32, STEPS, 128), F32),
            dma((5,)),
            dma((ARRAYS, 2)), dma((ARRAYS, 2)),
            dma((ARRAYS, 2)), dma((ARRAYS, 2)),
            dma((ARRAYS, 8)), dma((ARRAYS, 8)),
            dma((2, 2)), dma((2, 2)),
            dma, dma, dma, dma, dma, dma((ARRAYS, 2, 2)), dma((ARRAYS, 2, 2)),
        ],
        compiler_params=pltpu.CompilerParams(
            collective_id=0, has_side_effects=True, vmem_limit_bytes=60 << 20
        ),
        name="fdtd",
    )(pressure_new, pressure_old, codes, loss_table, receivers)
    return pl.pallas_call(
        hand_over,
        out_shape=shapes,
        in_specs=[vmem] * 2,
        out_specs=(vmem,) * 3,
        name="hand_over",
    )(*results)


def solution(mesh):
    in_specs = (P("gx", "gy", "gz"), P("gx", "gy", "gz"), P("gx", "gy", "gz"), P(), P())
    out_specs = (P("gx", "gy", "gz"), P("gx", "gy", "gz"), P())
    return jax.shard_map(
        on_device, mesh=mesh, in_specs=in_specs, out_specs=out_specs, check_vma=False
    )
```
